256 devices in a mesh: pts: 64 (over y, z, core), head: 4 (over x).
Axes of the slice: x: 4, y: 4, z: 8, core: 2. Of those that a mesh axis runs over, the one named last changes fastest.
Arguments:
- mesh_vertex_state: bfloat16 [524288, 256], P('pts'), may hold values from -6 to 6
- upstream_derivative: bfloat16 [524288, 256], P('pts'), may hold values from -6 to 6
- aggregate_mapping_matrix: bfloat16 [256, 256], P(None, 'head'), may hold values from -0.375 to 0.375
- partition_mapping_matrix: bfloat16 [256, 256], P(None, 'head'), may hold values from -0.375 to 0.375
- partition_score_matrix: bfloat16 [8, 32, 64], P('head'), may hold values from -1 to 1
- softmax_sharpness: float32 [8], P('head'), may hold values from 0.3 to 1
- query_key_value_maps: float32 [8, 3, 32, 32], P('head'), may hold values from -2 to 2
- final_mixing_matrix: bfloat16 [256, 256], P('head'), may hold values from -0.375 to 0.375
Outputs:
- input_grad: bfloat16 [524288, 256], P('pts', 'head')
- fx_weight_grad: float32 [256, 256], P(None, 'head')
- mid_weight_grad: float32 [256, 256], P(None, 'head')
- slice_weight_grad: float32 [8, 32, 64], P('head')
- attn_weight_grad: float32 [8, 3, 32, 32], P('head')
- out_weight_grad: float32 [256, 256], P('head')
The draws below stay inside these ranges and needn't reach their ends.
All inputs are finite; a program needn't handle non-finite values.
Results may differ from the reference program's by a relative error of at most 0.015.
Values may be sent and summed in bfloat16 or wider, within the bound.
No kernel may reach another device: no remote copies, remote signals or barrier semaphores. Data moves between devices by JAX's collectives and lax.ppermute only.
A program may use at most 128 MiB of HBM per device.

```python
import math
import jax
import jax.numpy as jnp
from jax import lax

WIDTH = 256
NUM_SUBSPACES = 8
HEAD_DIM = 32
SLICES = 64
POINTS = 524288


def shard_levels(own_key, extent, cuts, least, top_value):
    loudness, own = 1.0, jax.random.fold_in(own_key, 6)
    for position, parts in cuts:
        steps = jnp.exp(jax.random.uniform(jax.random.fold_in(own, position), (parts,), jnp.float32, least / len(cuts), top_value / len(cuts)))
        loudness = loudness * jnp.repeat(steps, extent[position] // parts).reshape([-1 if axis == position else 1 for axis in range(len(extent))])
    return loudness


def centred(key, dims, spread, reach, shards=(), held_as=jnp.bfloat16):
    level = shard_levels(key, dims, shards, -0.22, 0.18) if shards else 1.0
    entries = jax.random.normal(key, dims, jnp.float32) * spread * level
    return jnp.minimum(jnp.maximum(entries, -reach), reach).astype(held_as)


def setup_inputs(seed: int = 0) -> dict:
    seeds = jax.random.split(jax.random.key(seed), 9)
    mesh_vertex_state = centred(seeds[0], (POINTS, WIDTH), 1.0, 6.0, ((0, 64),))
    upstream_derivative = centred(seeds[1], (POINTS, WIDTH), 1.0, 6.0, ((0, 64),))
    aggregate_mapping_matrix = centred(seeds[2], (WIDTH, NUM_SUBSPACES * HEAD_DIM), WIDTH ** -0.5, 0.375, ((1, 4),))
    partition_mapping_matrix = centred(seeds[3], (WIDTH, NUM_SUBSPACES * HEAD_DIM), WIDTH ** -0.5, 0.375, ((1, 4),))
    partition_score_matrix = centred(seeds[4], (NUM_SUBSPACES, HEAD_DIM, SLICES), HEAD_DIM ** -0.5, 1.0, ((0, 4),))
    softmax_sharpness = jnp.clip(jnp.exp(math.log(1.0) - 1.2039728 * jax.random.uniform(seeds[5], (NUM_SUBSPACES,), jnp.float32) ** shard_levels(seeds[5], (NUM_SUBSPACES,), ((0, 4),), -0.2, 0.2)), 0.3, 1.0)
    query_key_value_maps = centred(seeds[6], (NUM_SUBSPACES, 3, HEAD_DIM, HEAD_DIM), (HEAD_DIM // 4) ** -0.5, 2.0, ((0, 4),), jnp.float32)
    final_mixing_matrix = centred(seeds[7], (NUM_SUBSPACES * HEAD_DIM, WIDTH), (NUM_SUBSPACES * HEAD_DIM) ** -0.5, 0.375, ((0, 4),))
    return dict(mesh_vertex_state=mesh_vertex_state, upstream_derivative=upstream_derivative, aggregate_mapping_matrix=aggregate_mapping_matrix, partition_mapping_matrix=partition_mapping_matrix, partition_score_matrix=partition_score_matrix, softmax_sharpness=softmax_sharpness, query_key_value_maps=query_key_value_maps, final_mixing_matrix=final_mixing_matrix)


HIGH = lax.Precision.HIGHEST

def fdot(left, right):
    return jnp.dot(left, right, precision=HIGH, preferred_element_type=jnp.float32)

def reference(mesh_vertex_state, upstream_derivative, aggregate_mapping_matrix, partition_mapping_matrix, partition_score_matrix, softmax_sharpness, query_key_value_maps, final_mixing_matrix):
    scale = 1.0 / math.sqrt(POINTS)
    root = 1.0 / math.sqrt(HEAD_DIM)
    input_acc = jnp.zeros((POINTS, WIDTH), jnp.float32)
    fx_list, mid_list, slice_list, attn_list, out_list = ([], [], [], [], [])
    for subspace_number in range(NUM_SUBSPACES):
        lo_col = subspace_number * HEAD_DIM
        w_feat = aggregate_mapping_matrix[:, lo_col:lo_col + HEAD_DIM]
        w_mid = partition_mapping_matrix[:, lo_col:lo_col + HEAD_DIM]
        feat = jnp.dot(mesh_vertex_state, w_feat, preferred_element_type=jnp.float32).astype(jnp.bfloat16)
        partition_inputs = jnp.dot(mesh_vertex_state, w_mid, preferred_element_type=jnp.float32).astype(jnp.bfloat16)
        partition_score = jnp.dot(partition_inputs, partition_score_matrix[subspace_number], preferred_element_type=jnp.float32) / softmax_sharpness[subspace_number]
        expo = jnp.exp(partition_score)
        parameter_tensors = expo / lax.optimization_barrier(jnp.sum(expo, axis=1, keepdims=True))
        weights_b = parameter_tensors.astype(jnp.bfloat16)
        pool = jnp.dot(weights_b.T, feat, preferred_element_type=jnp.float32)
        norm = lax.optimization_barrier(jnp.sum(parameter_tensors, axis=0))
        token = pool / norm[:, None]
        w_query, w_key, w_value = (query_key_value_maps[subspace_number, 0], query_key_value_maps[subspace_number, 1], query_key_value_maps[subspace_number, 2])
        query = fdot(token, w_query)
        keys_t = fdot(token, w_key)
        values_t = fdot(token, w_value)
        expo_s = jnp.exp(fdot(query, keys_t.T) * root)
        prob = expo_s / lax.optimization_barrier(jnp.sum(expo_s, axis=1, keepdims=True))
        slice_out = fdot(prob, values_t)
        slice_out_b = slice_out.astype(jnp.bfloat16)
        desliced = jnp.dot(weights_b, slice_out_b, preferred_element_type=jnp.float32).astype(jnp.bfloat16)
        w_out = final_mixing_matrix[lo_col:lo_col + HEAD_DIM]
        out_list.append(scale * jnp.dot(desliced.T, upstream_derivative, preferred_element_type=jnp.float32))
        grad_desliced = jnp.dot(upstream_derivative, w_out.T, preferred_element_type=jnp.float32).astype(jnp.bfloat16)
        grad_slice_out = jnp.dot(weights_b.T, grad_desliced, preferred_element_type=jnp.float32)
        grad_w1 = jnp.dot(grad_desliced, slice_out_b.T, preferred_element_type=jnp.float32)
        grad_prob = fdot(grad_slice_out, values_t.T)
        grad_value = fdot(prob.T, grad_slice_out)
        grad_score = prob * (grad_prob - lax.optimization_barrier(jnp.sum(prob * grad_prob, axis=1, keepdims=True))) * root
        grad_query = fdot(grad_score, keys_t)
        grad_key = fdot(grad_score.T, query)
        attn_list.append(jnp.stack([fdot(token.T, grad_query), fdot(token.T, grad_key), fdot(token.T, grad_value)]))
        grad_token = fdot(grad_query, w_query.T) + fdot(grad_key, w_key.T) + fdot(grad_value, w_value.T)
        grad_pool = (grad_token / norm[:, None]).astype(jnp.bfloat16)
        grad_norm = -lax.optimization_barrier(jnp.sum(grad_token * token, axis=1)) / norm
        parameter_derivative = grad_w1 + jnp.dot(feat, grad_pool.T, preferred_element_type=jnp.float32) + grad_norm[None, :]
        score_derivative = (parameter_tensors * (parameter_derivative - lax.optimization_barrier(jnp.sum(parameter_tensors * parameter_derivative, axis=1, keepdims=True))) / softmax_sharpness[subspace_number]).astype(jnp.bfloat16)
        grad_mid = jnp.dot(score_derivative, partition_score_matrix[subspace_number].T, preferred_element_type=jnp.float32).astype(jnp.bfloat16)
        grad_feat = jnp.dot(weights_b, grad_pool, preferred_element_type=jnp.float32).astype(jnp.bfloat16)
        slice_list.append(scale * jnp.dot(partition_inputs.T, score_derivative, preferred_element_type=jnp.float32))
        fx_list.append(jnp.dot(mesh_vertex_state.T, grad_feat, preferred_element_type=jnp.float32))
        mid_list.append(scale * jnp.dot(mesh_vertex_state.T, grad_mid, preferred_element_type=jnp.float32))
        input_acc = input_acc + jnp.dot(grad_feat, w_feat.T, preferred_element_type=jnp.float32)
        input_acc = input_acc + jnp.dot(grad_mid, w_mid.T, preferred_element_type=jnp.float32)
    return (input_acc.astype(jnp.bfloat16), jnp.concatenate(fx_list, axis=1), jnp.concatenate(mid_list, axis=1), jnp.stack(slice_list), jnp.stack(attn_list), jnp.concatenate(out_list, axis=0))
```

```python
import math

import jax
import jax.numpy as jnp
import numpy as np
from jax import lax
from jax.experimental import pallas as pl
from jax.experimental.pallas import tpu as pltpu
from jax.sharding import Mesh
from jax.sharding import PartitionSpec as P

HIGH = lax.Precision.HIGHEST
F32 = jnp.float32
BF16 = jnp.bfloat16
LOG2E = 1.4426950408889634
NN = (((1,), (0,)), ((), ()))
NT = (((1,), (1,)), ((), ()))
TN = (((0,), (0,)), ((), ()))
PTS = ("y", "z", "core")


def bdot(left, right, dims=NN):
    return lax.dot_general(left, right, dims, preferred_element_type=F32)


def fdot(left, right, dims=NN):
    return lax.dot_general(left, right, dims, precision=HIGH, preferred_element_type=F32)


def slice_weights(logits):
    rows, cols = logits.shape
    expo = jnp.exp2(logits).reshape(rows // 64, 64, cols)
    weights = expo * (1.0 / jnp.sum(expo, axis=1, keepdims=True))
    return weights.reshape(rows, cols)


def pool_kernel(sharp, x_ref, u_ref, wmid, ws, wfx, wout, pay_ref, ab_ref, mq_ref, mq, acc, nacc):
    step = pl.program_id(0)

    @pl.when(step == 0)
    def _():
        for h in range(2):
            full = bdot(ws[h], wmid[32 * h : 32 * h + 32, :], TN) * (LOG2E / sharp[h])
            high = full.astype(BF16)
            mq[64 * h : 64 * h + 64, :] = high
            mq[128 + 64 * h : 192 + 64 * h, :] = (full - high.astype(F32)).astype(BF16)
        acc[...] = jnp.zeros_like(acc)
        nacc[...] = jnp.zeros_like(nacc)

    rows = x_ref.shape[0]
    sub = 512
    for part in range(rows // sub):
        xs = x_ref[part * sub : part * sub + sub, :]
        us = u_ref[part * sub : part * sub + sub, :]
        both = bdot(mq[...], xs, NT)
        weights = slice_weights(both[:128] + both[128:])
        total = weights[:, :128]
        for tile in range(1, sub // 128):
            total = total + weights[:, 128 * tile : 128 * tile + 128]
        nacc[...] += total
        weights_b = weights.astype(BF16)
        acc[:, :256] += bdot(weights_b, xs)
        acc[:, 256:] += bdot(weights_b, us)

    @pl.when(step == pl.num_programs(0) - 1)
    def _():
        ab_ref[...] = acc[...]
        mq_ref[...] = mq[...]
        pool = fdot(wfx[...].astype(F32), acc[:, :256], NT)
        grad_out = fdot(wout[...].astype(F32), acc[:, 256:], NT)
        first = lax.broadcasted_iota(jnp.int32, (32, 128), 1) < 64
        pay_ref[0:32, :] = jnp.where(first, pool[:32], pool[32:])
        pay_ref[32:64, :] = jnp.where(first, grad_out[:32], grad_out[32:])
        norm = fdot(jnp.ones((16, 128), F32), nacc[...], NT)
        top = lax.broadcasted_iota(jnp.int32, (16, 128), 0) == 0
        pay_ref[64:80, :] = jnp.where(top, norm, 0.0)


def token_part(pay, h, sharp, qkv, ws, wmid, wfx, wout):
    lanes = slice(64 * h, 64 * h + 64)
    root = 1.0 / math.sqrt(32.0)
    norm = pay[64:65, lanes]
    token = pay[0:32, lanes] / norm
    grad_so = pay[32:64, lanes]
    maps = qkv[h]
    proj = fdot(maps, token)
    query, key, value = proj[:32], proj[32:64], proj[64:]
    expo = jnp.exp(fdot(key, query, TN) * root)
    prob = expo / jnp.sum(expo, axis=0, keepdims=True)
    so = fdot(value, prob)
    grad_prob = fdot(value, grad_so, TN)
    grad_value = fdot(grad_so, prob, NT)
    grad_score = prob * (grad_prob - jnp.sum(prob * grad_prob, axis=0, keepdims=True)) * root
    grad_query = fdot(key, grad_score)
    grad_key = fdot(query, grad_score, NT)
    grads = jnp.concatenate([grad_query, grad_key, grad_value], axis=0)
    attn = fdot(token, grads, NT)
    grad_token = fdot(maps, grads, TN)
    grad_pool = (grad_token / norm).astype(BF16)
    grad_norm = -fdot(grad_token * token / norm, jnp.ones((32, 128), F32), TN)
    return so.astype(BF16), grad_pool, grad_norm, attn


def centre(block):
    return block - jnp.mean(block, axis=0, keepdims=True)


def grad_kernel(
    scale, sharp, me, pay, qkv, ws, wmid, wfx, wout, ab, mq, x_ref, u_ref,
    out0, out1, out2, out3, grads_ref, attn_ref,
    mx, mu, gn, wc, wcr, sob, gpb, gacc,
):
    step = pl.program_id(0)

    @pl.when(step == 0)
    def _():
        mx[0:256, :] = mq[...]
        for h in range(2):
            feat = slice(32 * h, 32 * h + 32)
            rows = slice(64 * h, 64 * h + 64)
            so, grad_pool, grad_norm, attn = token_part(pay, h, sharp, qkv, ws, wmid, wfx, wout)
            sob[feat, :] = so
            gpb[feat, :] = grad_pool
            for j in range(3):
                attn_ref[h, j] = attn[:, 32 * j : 32 * j + 32]
            inv = 1.0 / sharp[h]
            mu[rows, :] = (centre(bdot(so, wout[feat, :], TN)) * inv).astype(BF16)
            mx[256 + 64 * h : 320 + 64 * h, :] = (
                centre(bdot(grad_pool, wfx[feat, :], TN)) * inv
            ).astype(BF16)
            gn[rows, :] = grad_norm * inv
            wc[:, 64 * h : 64 * h + 64] = bdot(wmid[feat, :], ws[h], TN).astype(BF16)
            wc[:, 128 + 64 * h : 192 + 64 * h] = bdot(wfx[feat, :], grad_pool, TN).astype(BF16)
        for k in range(4):
            group = lax.rem(me[0] + k, 4)
            wcr[64 * k : 64 * k + 64, :] = wc[pl.ds(pl.multiple_of(group * 64, 64), 64), :]
        gacc[...] = jnp.zeros_like(gacc)

    rows = x_ref.shape[0]
    sub = 512
    for part in range(rows // sub):
        here = slice(part * sub, part * sub + sub)
        xs = x_ref[here, :]
        us = u_ref[here, :]
        both = bdot(mx[...], xs, NT)
        weights = slice_weights(both[:128] + both[128:256])
        grad_w = both[256:] + bdot(mu[...], us, NT) + gn[:, :1]
        prod = (weights * grad_w).reshape(2, 64, sub)
        mean = jnp.sum(prod, axis=1, keepdims=True)
        grad_logit = (prod - weights.reshape(2, 64, sub) * mean).reshape(128, sub).astype(BF16)
        gacc[...] += bdot(grad_logit, xs)
        pair = jnp.concatenate([grad_logit, weights.astype(BF16)], axis=0)
        out = bdot(wcr[...], pair).astype(BF16)
        for k, ref in enumerate((out0, out1, out2, out3)):
            ref[:, here] = out[64 * k : 64 * k + 64]

    @pl.when(step == pl.num_programs(0) - 1)
    def _():
        for h in range(2):
            feat = slice(32 * h, 32 * h + 32)
            rows = slice(64 * h, 64 * h + 64)
            grads_ref[feat, :] = fdot(gpb[feat, :].astype(F32), ab[rows, :256])
            grads_ref[64 + 32 * h : 96 + 32 * h, :] = scale * fdot(ws[h].astype(F32), gacc[rows, :])
            grads_ref[128 + 32 * h : 160 + 32 * h, :] = scale * fdot(
                sob[feat, :].astype(F32), ab[rows, 256:]
            )
        score = scale * fdot(wmid[...].astype(F32), gacc[...], NT)
        first = lax.broadcasted_iota(jnp.int32, (32, 128), 1) < 64
        score = jnp.where(first, score[:32], score[32:])
        grads_ref[192:208, :128] = score[:16]
        grads_ref[192:208, 128:] = score[16:]


def whole(shape):
    return pl.BlockSpec(shape, lambda i: (0,) * len(shape))


SMEM = pl.BlockSpec(memory_space=pltpu.SMEM)


def first_pass(sharp, x, u, wmid, ws, wfx, wout, block=1024):
    points = x.shape[0]
    rows = pl.BlockSpec((block, 256), lambda i: (i, 0))
    return pl.pallas_call(
        pool_kernel,
        grid=(points // block,),
        in_specs=[SMEM, rows, rows, whole((64, 256)), whole((2, 32, 64)), whole((64, 256)), whole((64, 256))],
        out_specs=[whole((80, 128)), whole((128, 512)), whole((256, 256))],
        out_shape=[
            jax.ShapeDtypeStruct((80, 128), F32),
            jax.ShapeDtypeStruct((128, 512), F32),
            jax.ShapeDtypeStruct((256, 256), BF16),
        ],
        scratch_shapes=[
            pltpu.VMEM((256, 256), BF16),
            pltpu.VMEM((128, 512), F32),
            pltpu.VMEM((128, 128), F32),
        ],
        compiler_params=pltpu.CompilerParams(vmem_limit_bytes=32 * 1024 * 1024),
        name="pool_pass",
    )(sharp, x, u, wmid, ws, wfx, wout)


def second_pass(scale, sharp, me, pay, qkv, ws, wmid, wfx, wout, ab, mq, x, u, block=1024):
    points = x.shape[0]
    rows = pl.BlockSpec((block, 256), lambda i: (i, 0))
    cols = pl.BlockSpec((64, block), lambda i: (0, i))

    def kernel(*refs):
        grad_kernel(scale, *refs)

    return pl.pallas_call(
        kernel,
        grid=(points // block,),
        in_specs=[
            SMEM, SMEM, whole((80, 128)), whole((2, 96, 32)), whole((2, 32, 64)), whole((64, 256)),
            whole((64, 256)), whole((64, 256)), whole((128, 512)), whole((256, 256)), rows, rows,
        ],
        out_specs=[cols] * 4 + [whole((208, 256)), whole((2, 3, 32, 32))],
        out_shape=[jax.ShapeDtypeStruct((64, points), BF16)] * 4
        + [
            jax.ShapeDtypeStruct((208, 256), F32),
            jax.ShapeDtypeStruct((2, 3, 32, 32), F32),
        ],
        scratch_shapes=[
            pltpu.VMEM((384, 256), BF16),
            pltpu.VMEM((128, 256), BF16),
            pltpu.VMEM((128, 128), F32),
            pltpu.VMEM((256, 256), BF16),
            pltpu.VMEM((256, 256), BF16),
            pltpu.VMEM((64, 64), BF16),
            pltpu.VMEM((64, 64), BF16),
            pltpu.VMEM((128, 256), F32),
        ],
        compiler_params=pltpu.CompilerParams(vmem_limit_bytes=32 * 1024 * 1024),
        name="grad_pass",
    )(sharp, me, pay, qkv, ws, wmid, wfx, wout, ab, mq, x, u)


def core_swap(value):
    return lax.ppermute(value, "core", [(0, 1), (1, 0)])


def core_scatter(value):
    core = lax.axis_index("core")
    half = value.shape[0] // 2
    mine = lax.dynamic_slice_in_dim(value, core * half, half)
    other = lax.dynamic_slice_in_dim(value, (1 - core) * half, half)
    return mine + core_swap(other)


def core_gather(value):
    core = lax.axis_index("core")
    other = core_swap(value)
    return jnp.concatenate(
        [jnp.where(core == 0, value, other), jnp.where(core == 0, other, value)], axis=0
    )


def y_sum(value, size, kind=F32):
    parts = [
        lax.ppermute(value, "y", [(i, i ^ k) for i in range(size)]).astype(kind)
        for k in range(1, size)
    ]
    return (value.astype(kind) + parts[0]) + (parts[1] + parts[2])


def z_sum(value, size, kind=F32):
    sent = jnp.broadcast_to(value[None], (size,) + value.shape)
    return jnp.sum(lax.all_to_all(sent, "z", 0, 0).astype(kind), axis=0)


def sum_points(value, sizes):
    half = core_scatter(value)
    half = y_sum(half, sizes["y"])
    half = z_sum(half, sizes["z"])
    return core_gather(half)


def sum_points_16(value, sizes):
    half = core_scatter(value).astype(BF16)
    half = y_sum(half, sizes["y"]).astype(BF16)
    half = z_sum(half, sizes["z"])
    return core_gather(half)


def solution(mesh):
    sizes = {"y": 4, "z": 8, "core": 2, "head": 4}
    fine = Mesh(np.asarray(mesh.devices).reshape(tuple(sizes.values())), tuple(sizes))

    def per_device(x, u, wfx, wmid, ws, sharp, qkv, wout):
        points = x.shape[0]
        scale = 1.0 / math.sqrt(points * 64)
        wfx_t = wfx.T
        wmid_t = wmid.T
        maps = jnp.swapaxes(qkv, 2, 3).reshape(2, 96, 32)
        pay, ab, mq = first_pass(sharp, x, u, wmid_t, ws, wfx_t, wout)
        pay = sum_points(pay, sizes)
        me = lax.axis_index("head").astype(jnp.int32).reshape(1)
        out0, out1, out2, out3, grads, attn = second_pass(
            scale, sharp, me, pay, maps, ws, wmid_t, wfx_t, wout, ab, mq, x, u
        )
        received = [
            lax.ppermute(part, "head", [(i, (i + k) % 4) for i in range(4)])
            for k, part in ((1, out1), (2, out2), (3, out3))
        ]
        grads = sum_points_16(grads, sizes)
        total = out0.astype(F32)
        for part in received:
            total = total + part.astype(F32)
        score = jnp.concatenate([grads[192:, :128], grads[192:, 128:]], axis=0)
        slice_grad = score.reshape(32, 2, 64).transpose(1, 0, 2)
        return (
            total.astype(BF16).T,
            grads[0:64].T,
            grads[64:128].T,
            slice_grad,
            attn,
            grads[128:192],
        )

    in_specs = (
        P(PTS, None),
        P(PTS, None),
        P(None, "head"),
        P(None, "head"),
        P("head", None, None),
        P("head"),
        P("head", None, None, None),
        P("head", None),
    )
    out_specs = (
        P(PTS, "head"),
        P(None, "head"),
        P(None, "head"),
        P("head", None, None),
        P("head", None, None, None),
        P("head", None),
    )
    return jax.shard_map(
        per_device, mesh=fine, in_specs=in_specs, out_specs=out_specs, check_vma=False
    )
```

```python
import math
import jax
import jax.numpy as jnp
import numpy as np
from jax import lax
from jax.experimental import pallas as pl
from jax.experimental.pallas import tpu as pltpu
from jax.sharding import Mesh
from jax.sharding import PartitionSpec as P

HIGH = lax.Precision.HIGHEST
F32 = jnp.float32
BF16 = jnp.bfloat16
LOG2E = 1.4426950408889634
PTS = ("y", "z", "core")
NN = (((1,), (0,)), ((), ()))
NT = (((1,), (1,)), ((), ()))
TN = (((0,), (0,)), ((), ()))
LIMIT = 24 * 1024 * 1024


def bdot(left, right, dims=NN):
    return lax.dot_general(left, right, dims, preferred_element_type=F32)


def fdot(left, right, dims=NN):
    return lax.dot_general(left, right, dims, precision=HIGH, preferred_element_type=F32)


def slice_weights(logits):
    rows, cols = logits.shape
    expo = jnp.exp2(logits).reshape(rows // 64, 64, cols)
    weights = expo * (1.0 / jnp.sum(expo, axis=1, keepdims=True))
    return weights.reshape(rows, cols)


def start_rows(pairs, sems, cuts):
    waits = []
    for k, (lo, hi) in enumerate(cuts):
        copies = [
            pltpu.make_async_copy(src.at[lo:hi, :], dst.at[lo:hi, :], sems.at[j, k])
            for j, (src, dst) in enumerate(pairs)
        ]
        for copy in copies:
            copy.start()
        waits.append(copies)
    return waits


def pool_kernel(
    cuts, sub, me, sharp, x_hbm, u_hbm, wmid, ws, wfx, wout,
    mine_ref, rest_ref, ab_ref, mq, x, u, pay, nacc, sems,
):
    waits = start_rows(((x_hbm, x), (u_hbm, u)), sems, cuts)
    for h in range(2):
        full = bdot(ws[h], wmid[32 * h : 32 * h + 32, :], TN) * (LOG2E / sharp[h])
        high = full.astype(BF16)
        mq[64 * h : 64 * h + 64, :] = high
        mq[128 + 64 * h : 192 + 64 * h, :] = (full - high.astype(F32)).astype(BF16)
    ab_ref[...] = jnp.zeros_like(ab_ref)
    nacc[...] = jnp.zeros_like(nacc)
    for (first, last), copies in zip(cuts, waits):
        for copy in copies:
            copy.wait()
        for lo in range(first, last, sub):
            xs = x[lo : lo + sub, :]
            both = bdot(mq[...], xs, NT)
            weights = slice_weights(both[:128] + both[128:])
            total = weights[:, :128]
            for tile in range(1, sub // 128):
                total = total + weights[:, 128 * tile : 128 * tile + 128]
            nacc[...] += total
            weights_b = weights.astype(BF16)
            ab_ref[:, :256] += bdot(weights_b, xs)
            ab_ref[:, 256:] += bdot(weights_b, u[lo : lo + sub, :])
    pool = fdot(wfx[...].astype(F32), ab_ref[:, :256], NT)
    grad_out = fdot(wout[...].astype(F32), ab_ref[:, 256:], NT)
    first = lax.broadcasted_iota(jnp.int32, (32, 128), 1) < 64
    pay[0:32, :] = jnp.where(first, pool[:32], pool[32:])
    pay[32:64, :] = jnp.where(first, grad_out[:32], grad_out[32:])
    norm = fdot(jnp.ones((16, 128), F32), nacc[...], NT)
    top = lax.broadcasted_iota(jnp.int32, (16, 128), 0) == 0
    pay[64:80, :] = jnp.where(top, norm, 0.0)
    split_rows(me[1], pay, mine_ref, rest_ref)


def split_rows(core, value, mine, rest):
    half = mine.shape[0]
    mine[...] = value[pl.ds(pl.multiple_of(core * half, 8), half), :]
    rest[...] = value[pl.ds(pl.multiple_of((1 - core) * half, 8), half), :]


def token_part(pay, h, qkv):
    lanes = slice(64 * h, 64 * h + 64)
    root = 1.0 / math.sqrt(32.0)
    norm = pay[64:65, lanes]
    token = pay[0:32, lanes] / norm
    grad_so = pay[32:64, lanes]
    maps = jnp.concatenate([qkv[h, 0], qkv[h, 1], qkv[h, 2]], axis=1)
    proj = fdot(maps, token, TN)
    query, key, value = proj[:32], proj[32:64], proj[64:]
    expo = jnp.exp(fdot(key, query, TN) * root)
    prob = expo / jnp.sum(expo, axis=0, keepdims=True)
    so = fdot(value, prob)
    grad_prob = fdot(value, grad_so, TN)
    grad_value = fdot(grad_so, prob, NT)
    grad_score = prob * (grad_prob - jnp.sum(prob * grad_prob, axis=0, keepdims=True)) * root
    grad_query = fdot(key, grad_score)
    grad_key = fdot(query, grad_score, NT)
    grads = jnp.concatenate([grad_query, grad_key, grad_value], axis=0)
    attn = fdot(token, grads, NT)
    grad_token = fdot(maps, grads)
    grad_pool = (grad_token / norm).astype(BF16)
    grad_norm = -jnp.sum(grad_token * token, axis=0, keepdims=True) / norm
    return so.astype(BF16), grad_pool, grad_norm, attn


def centre(block):
    rows, cols = block.shape
    heads = block.reshape(rows // 64, 64, cols)
    return (heads - jnp.mean(heads, axis=1, keepdims=True)).reshape(rows, cols)


def split3(value):
    high = value.astype(BF16)
    rest = value - high.astype(F32)
    mid = rest.astype(BF16)
    return high, mid, (rest - mid.astype(F32)).astype(BF16)


def token_kernel(
    me, sharp, half, other, qkv, ws, wmid, wfx, wout, pack, attn_ref, mu_ref, mx_ref, gn_ref, pay,
):
    rows = half.shape[0]
    pay[pl.ds(pl.multiple_of(me[1] * rows, 8), rows), :] = half[...]
    pay[pl.ds(pl.multiple_of((1 - me[1]) * rows, 8), rows), :] = other[...]
    pack[0:80, :] = jnp.zeros((80, 256), BF16)
    pack[80:144, :] = wfx[...]
    pack[144:208, :] = wmid[...]
    pack[208:272, :] = wout[...]
    pack[272:336, :] = jnp.zeros((64, 256), BF16)
    for h in range(2):
        feat = slice(32 * h, 32 * h + 32)
        so, grad_pool, grad_norm, attn = token_part(pay, h, qkv)
        for j in range(3):
            attn_ref[h, j] = attn[:, 32 * j : 32 * j + 32]
        pack[feat, 64 * h : 64 * h + 64] = so
        pack[feat, 128 + 64 * h : 192 + 64 * h] = grad_pool
        pack[272 + 32 * h : 304 + 32 * h, 64 * h : 64 * h + 64] = ws[h]
        inv = 1.0 / (jnp.zeros((1, 64), F32) + sharp[h])
        parts = split3(grad_norm) + split3(inv)
        rows = [p for p in parts] + [jnp.zeros((10, 64), BF16)]
        pack[64:80, 64 * h : 64 * h + 64] = jnp.concatenate(rows, axis=0)
    mu, mx, _, gn = unpack_maps(pack, wfx[...], wout[...])
    mu_ref[...] = mu
    mx_ref[...] = mx
    gn_ref[...] = gn


def unpack_maps(pack, wfx, wout):
    pick = lax.broadcasted_iota(jnp.int32, (16, 256), 0)
    lane = lax.broadcasted_iota(jnp.int32, (16, 256), 1)
    first = jnp.where(lane < 128, 0, 3)
    chosen = jnp.where((pick >= first) & (pick < first + 3), 1.0, 0.0).astype(BF16)
    cols = bdot(pack[64:80, 0:128], chosen, TN)
    inv = cols[:, 128:]
    gn = cols[:, :128] * inv
    mu = centre(bdot(pack[0:64, 0:128], wout, TN)) * inv[:, :1]
    mx = centre(bdot(pack[0:64, 128:256], wfx, TN)) * inv[:, :1]
    return mu.astype(BF16), mx.astype(BF16), inv, gn


def logit_grad(weights, grad_w):
    rows, cols = weights.shape
    prod = (weights * grad_w).reshape(rows // 64, 64, cols)
    mean = jnp.sum(prod, axis=1, keepdims=True)
    grad = prod - weights.reshape(rows // 64, 64, cols) * mean
    return grad.reshape(rows, cols).astype(BF16)


def weight_kernel(
    scale, sub, unroll, me, wmid, ws, pack, ab, mq, mu, mx, gn, x, u, mine, rest, grads_ref, maps, gacc,
):
    points=x.shape[0]
    maps[0:256, :] = mq[...]
    maps[256:384, :] = mx[...]
    gacc[...] = jnp.zeros_like(gacc)
    def one(lo):
        here=pl.ds(lo,sub)
        xs = x[here, :]
        both = bdot(maps[...], xs, NT)
        weights = slice_weights(both[:128] + both[128:256])
        grad_w = both[256:] + bdot(mu[...], u[here, :], NT) + gn[:, :1]
        gacc[...] += bdot(logit_grad(weights, grad_w), xs)
    n=points//sub
    def body(i,_):
        for j in range(unroll): one(pl.multiple_of((i*unroll+j)*sub,sub))
        return 0
    if unroll==n: body(0,0)
    else: lax.fori_loop(0,n//unroll,body,0)
    so = pack[0:64, 0:128].astype(F32)
    grad_pool = pack[0:64, 128:256].astype(F32)
    grads_ref[0:64, :] = fdot(grad_pool, ab[:, :256])
    for h in range(2):
        grads_ref[64 + 32 * h : 96 + 32 * h, :] = scale * fdot(
            ws[h].astype(F32), gacc[64 * h : 64 * h + 64, :]
        )
    grads_ref[128:192, :] = scale * fdot(so, ab[:, 256:])
    score = scale * fdot(wmid[...].astype(F32), gacc[...], NT)
    first = lax.broadcasted_iota(jnp.int32, (32, 128), 1) < 64
    score = jnp.where(first, score[:32], score[32:])
    grads_ref[192:208, :128] = score[:16]
    grads_ref[192:208, 128:] = score[16:]
    split_rows(me[1], grads_ref, mine, rest)

def input_kernel(
    sub, unroll, me, p0, p1, p2, p3, x, u, out0, out1, out2, out3,
    qx, mu, gn, wc, wcr,
):
    points = out0.shape[1]
    for g, pack in enumerate((p0, p1, p2, p3)):
        rows = slice(128 * g, 128 * g + 128)
        wfx = pack[80:144, :]
        wmid = pack[144:208, :]
        score_map = pack[272:336, 0:128]
        mu_g, mx_g, inv, gn_g = unpack_maps(pack, wfx, pack[208:272, :])
        full = bdot(score_map, wmid, TN) * (LOG2E * inv[:, :1])
        high = full.astype(BF16)
        qx[rows, :] = high
        qx[512 + 128 * g : 640 + 128 * g, :] = (full - high.astype(F32)).astype(BF16)
        qx[1024 + 128 * g : 1152 + 128 * g, :] = mx_g
        mu[rows, :] = mu_g
        gn[rows, :] = gn_g
        wc[:, rows] = bdot(wmid, score_map, TN).astype(BF16)
        wc[:, 512 + 128 * g : 640 + 128 * g] = bdot(wfx, pack[0:64, 128:256], TN).astype(BF16)
    for k in range(4):
        group = lax.rem(me[0] + k, 4)
        wcr[64 * k : 64 * k + 64, :] = wc[pl.ds(pl.multiple_of(group * 64, 64), 64), :]
    def one(lo):
        here = pl.ds(pl.multiple_of(me[0] * points + lo, sub), sub)
        both = bdot(qx[...], x[here, :], NT)
        weights = slice_weights(both[:512] + both[512:1024])
        grad_w = both[1024:] + bdot(mu[...], u[here, :], NT) + gn[:, :1]
        pair = jnp.concatenate([logit_grad(weights, grad_w), weights.astype(BF16)], axis=0)
        out = bdot(wcr[...], pair).astype(BF16)
        for k, ref in enumerate((out0, out1, out2, out3)):
            ref[:, pl.ds(lo,sub)] = out[64 * k : 64 * k + 64]
    n=points//sub
    def body(i,_):
        for j in range(unroll): one(pl.multiple_of((i*unroll+j)*sub,sub))
        return 0
    if unroll==n: body(0,0)
    else: lax.fori_loop(0,n//unroll,body,0)

SMEM = pl.BlockSpec(memory_space=pltpu.SMEM)
VM = pl.BlockSpec(memory_space=pltpu.VMEM)
HB = pl.BlockSpec(memory_space=pltpu.HBM)
PARAMS = pltpu.CompilerParams(vmem_limit_bytes=LIMIT)


def cost(flops):
    return pl.CostEstimate(flops=flops, bytes_accessed=1 << 23, transcendentals=0)


def first_pass(me, sharp, x, u, wmid, ws, wfx, wout, chunks=4, sub=256):
    points = x.shape[0]
    size = points // chunks
    cuts = [(size * i, size * i + size) for i in range(chunks)]

    def kernel(*refs):
        pool_kernel(cuts, sub, *refs)

    return pl.pallas_call(
        kernel,
        in_specs=[SMEM, SMEM, HB, HB, VM, VM, VM, VM],
        out_specs=[VM] * 6,
        out_shape=[
            jax.ShapeDtypeStruct((40, 128), F32),
            jax.ShapeDtypeStruct((40, 128), F32),
            jax.ShapeDtypeStruct((128, 512), F32),
            jax.ShapeDtypeStruct((256, 256), BF16),
            jax.ShapeDtypeStruct(x.shape, BF16),
            jax.ShapeDtypeStruct(u.shape, BF16),
        ],
        scratch_shapes=[
            pltpu.VMEM((80, 128), F32),
            pltpu.VMEM((128, 128), F32),
            pltpu.SemaphoreType.DMA((2, len(cuts))),
        ],
        compiler_params=PARAMS,
        cost_estimate=cost(1 << 33),
        name="pool_pass",
    )(me, sharp, x, u, wmid, ws, wfx, wout)


def token_pass(me, sharp, half, other, qkv, ws, wmid, wfx, wout):
    return pl.pallas_call(
        token_kernel,
        in_specs=[SMEM, SMEM] + [VM] * 7,
        out_specs=[VM] * 5,
        out_shape=[
            jax.ShapeDtypeStruct((336, 256), BF16),
            jax.ShapeDtypeStruct((2, 3, 32, 32), F32),
            jax.ShapeDtypeStruct((128, 256), BF16),
            jax.ShapeDtypeStruct((128, 256), BF16),
            jax.ShapeDtypeStruct((128, 128), F32),
        ],
        scratch_shapes=[pltpu.VMEM((80, 128), F32)],
        compiler_params=PARAMS,
        name="token_pass",
    )(me, sharp, half, other, qkv, ws, wmid, wfx, wout)


def weight_pass(me, scale, wmid, ws, pack, ab, mq, mu, mx, gn, x, u, sub=512, unroll=8):
    def kernel(*refs):
        weight_kernel(scale, sub, unroll, *refs)

    return pl.pallas_call(
        kernel,
        in_specs=[SMEM] + [VM] * 10,
        out_specs=[VM] * 2,
        out_shape=[jax.ShapeDtypeStruct((104, 256), F32)] * 2,
        scratch_shapes=[
            pltpu.VMEM((208, 256), F32),
            pltpu.VMEM((384, 256), BF16),
            pltpu.VMEM((128, 256), F32),
        ],
        compiler_params=PARAMS,
        cost_estimate=cost(1 << 33),
        name="weight_pass",
    )(me, wmid, ws, pack, ab, mq, mu, mx, gn, x, u)


def input_pass(me, packs, x, u, sub=512, unroll=4):
    points = x.shape[0] // 4

    def kernel(*refs):
        input_kernel(sub, unroll, *refs)

    return pl.pallas_call(
        kernel,
        in_specs=[SMEM] + [VM] * 6,
        out_specs=[VM] * 4,
        out_shape=[jax.ShapeDtypeStruct((64, points), BF16)] * 4,
        scratch_shapes=[
            pltpu.VMEM((1536, 256), BF16),
            pltpu.VMEM((512, 256), BF16),
            pltpu.VMEM((512, 128), F32),
            pltpu.VMEM((256, 1024), BF16),
            pltpu.VMEM((256, 1024), BF16),
        ],
        compiler_params=PARAMS,
        cost_estimate=cost(1 << 33),
        name="input_pass",
    )(me, *packs, x, u)


def final_kernel(me, half, other, part0, part1, part2, part3, fx, mid, out, score, grad, grads, sems):
    copies = []
    for k, part in enumerate((part0, part1, part2, part3)):
        group = lax.rem(me[0] + 4 - k, 4)
        size = part.shape[1]
        place = grad.at[:, pl.ds(pl.multiple_of(group * size, size), size)]
        copies.append(pltpu.make_async_copy(part, place, sems.at[k]))
        copies[-1].start()
    rows = half.shape[0]
    grads[pl.ds(pl.multiple_of(me[1] * rows, 8), rows), :] = half[...]
    grads[pl.ds(pl.multiple_of((1 - me[1]) * rows, 8), rows), :] = other[...]
    fx[...] = grads[0:64, :]
    mid[...] = grads[64:128, :]
    out[...] = grads[128:192, :]
    for h in range(2):
        for j in range(2):
            score[h, 16 * j : 16 * j + 16, :] = grads[
                192:208, 128 * j + 64 * h : 128 * j + 64 * h + 64
            ]
    for copy in copies:
        copy.wait()


def final_pass(me, half, other, parts):
    size = parts[0].shape[1]
    flat = jax.ShapeDtypeStruct((64, 256), F32)
    return pl.pallas_call(
        final_kernel,
        in_specs=[SMEM] + [VM] * 6,
        out_specs=[VM] * 4 + [HB],
        out_shape=[flat, flat, flat]
        + [
            jax.ShapeDtypeStruct((2, 32, 64), F32),
            jax.ShapeDtypeStruct((64, 4 * size), BF16),
        ],
        scratch_shapes=[pltpu.VMEM((208, 256), F32), pltpu.SemaphoreType.DMA((4,))],
        compiler_params=PARAMS,
        name="final_pass",
    )(me, half, other, *parts)


def core_swap(value):
    return lax.ppermute(value, "core", [(0, 1), (1, 0)])


def y_sum(value):
    parts = [
        lax.ppermute(value, "y", [(i, i ^ k) for i in range(4)]).astype(F32) for k in range(1, 4)
    ]
    return (value.astype(F32) + parts[0]) + (parts[1] + parts[2])


def z_sum(value):
    sent = jnp.broadcast_to(value[None], (8,) + value.shape)
    got = lax.all_to_all(sent, "z", 0, 0).astype(F32)
    total = got[0]
    for part in range(1, 8):
        total = total + got[part]
    return total


def shifted(value, k):
    return lax.ppermute(value, "head", [(i, (i + k) % 4) for i in range(4)])


def per_device(x, u, wfx, wmid, ws, sharp, qkv, wout):
    points = x.shape[0]
    scale = 1.0 / math.sqrt(points * 64)
    me = jnp.stack([lax.axis_index("head"), lax.axis_index("core")]).astype(jnp.int32)
    wfx = wfx.T
    wmid = wmid.T
    held = [
        pltpu.with_memory_space_constraint(v, pltpu.HBM) for v in (sharp, x, u, wmid, ws, wfx, wout)
    ]
    mine, rest, ab, mq, x, u = first_pass(me, *held)
    half = z_sum(y_sum(mine + core_swap(rest)))
    pack, attn, mu, mx, gn = token_pass(
        me, sharp, half, core_swap(half), qkv, ws, wmid, wfx, wout
    )
    packs = [pack] + [shifted(pack, k) for k in (1, 2, 3)]
    mine, rest = weight_pass(me, scale, wmid, ws, pack, ab, mq, mu, mx, gn, x, u)
    mine, rest, packs = lax.optimization_barrier((mine, rest, packs))
    half = y_sum((mine + core_swap(rest)).astype(BF16)).astype(BF16)
    parts = input_pass(me, packs, x, u)
    half, parts = lax.optimization_barrier((half, parts))
    parts = [parts[0]] + [shifted(parts[k], k) for k in (1, 2, 3)]
    half = z_sum(half)
    fx, mid, out, score, grad = final_pass(me, half, core_swap(half), parts)
    return grad.T, fx.T, mid.T, score, attn, out


def solution(mesh):
    fine = Mesh(np.asarray(mesh.devices).reshape(4, 8, 2, 4), PTS + ("head",))
    in_specs = (
        P(PTS, None),
        P(PTS, None),
        P(None, "head"),
        P(None, "head"),
        P("head", None, None),
        P("head"),
        P("head", None, None, None),
        P("head", None),
    )
    out_specs = (
        P(PTS, "head"),
        P(None, "head"),
        P(None, "head"),
        P("head", None, None),
        P("head", None, None, None),
        P("head", None),
    )
    return jax.shard_map(
        per_device, mesh=fine, in_specs=in_specs, out_specs=out_specs, check_vma=False
    )
```

```python
import math

import jax
import jax.numpy as jnp
import numpy as np
from jax import lax
from jax.experimental import pallas as pl
from jax.experimental.pallas import tpu as pltpu
from jax.sharding import Mesh
from jax.sharding import PartitionSpec as P

F32 = jnp.float32
BF16 = jnp.bfloat16
LOG2E = 1.4426950408889634
PTS = ("y", "z", "core")
NN = (((1,), (0,)), ((), ()))
NT = (((1,), (1,)), ((), ()))
TN = (((0,), (0,)), ((), ()))
SMEM = pl.BlockSpec(memory_space=pltpu.SMEM)
VM = pl.BlockSpec(memory_space=pltpu.VMEM)
HB = pl.BlockSpec(memory_space=pltpu.HBM)
PARAMS = pltpu.CompilerParams(vmem_limit_bytes=24 * 1024 * 1024)
PACK = (144, 256)


def bdot(left, right, dims=NN):
    return lax.dot_general(left, right, dims, preferred_element_type=F32)


def halves(value):
    high = value.astype(BF16)
    return high, (value - high.astype(F32)).astype(BF16)


def edot(exact, value, dims=NN):
    high, low = halves(value)
    return bdot(exact, high, dims) + bdot(exact, low, dims)


def fdot(left, right, dims=NN):
    left_high, left_low = halves(left)
    right_high, right_low = halves(right)
    return (bdot(left_high, right_low, dims) + bdot(left_low, right_high, dims)) + bdot(
        left_high, right_high, dims
    )


def slice_weights(logits):
    expo = jnp.exp2(logits)
    return expo * (1.0 / jnp.sum(expo, axis=0, keepdims=True))


def all_weights(logits):
    rows, cols = logits.shape
    expo = jnp.exp2(logits).reshape(rows // 64, 64, cols)
    weights = expo * (1.0 / jnp.sum(expo, axis=1, keepdims=True))
    return weights.reshape(rows, cols)


def all_logit_grads(weights, grad_w):
    rows, cols = weights.shape
    weights = weights.reshape(rows // 64, 64, cols)
    prod = weights * grad_w.reshape(rows // 64, 64, cols)
    grad = prod - weights * jnp.sum(prod, axis=1, keepdims=True)
    return grad.reshape(rows, cols).astype(BF16)


def logit_grad(weights, grad_w):
    mean = jnp.sum(weights * grad_w, axis=0, keepdims=True)
    return (weights * (grad_w - mean)).astype(BF16)


def tiles(heads, cols, width):
    for h in range(heads):
        for lo in range(0, cols, width):
            yield slice(64 * h, 64 * h + 64), slice(lo, lo + width)


def row_copies(x_hbm, u_hbm, xu, sems, chunk):
    def copies(i):
        rows = pl.ds(pl.multiple_of(i * chunk, chunk), chunk)
        return [
            pltpu.make_async_copy(
                src.at[rows, :], xu.at[rows, 256 * j : 256 * j + 256], sems.at[j, i]
            )
            for j, src in enumerate((x_hbm, u_hbm))
        ]

    def start(i):
        for copy in copies(i):
            copy.start()

    def wait(i):
        for copy in copies(i):
            copy.wait()

    return start, wait


def pool_kernel(
    chunk, sub, me, sharp, x_hbm, u_hbm, wmid, ws, wfx, wout,
    mine_ref, rest_ref, ab_ref, mq, x, u, pay, nacc, sems,
):
    waits = []
    for k, lo in enumerate(range(0, x.shape[0], chunk)):
        copies = [
            pltpu.make_async_copy(src.at[lo : lo + chunk, :], dst.at[lo : lo + chunk, :], sems.at[j, k])
            for j, (src, dst) in enumerate(((x_hbm, x), (u_hbm, u)))
        ]
        for copy in copies:
            copy.start()
        waits.append(copies)
    ab_ref[...] = jnp.zeros_like(ab_ref)
    nacc[...] = jnp.zeros_like(nacc)
    for h in range(2):
        full = bdot(ws[h], wmid[32 * h : 32 * h + 32, :], TN) * (LOG2E / sharp[h])
        mq[64 * h : 64 * h + 64, :], mq[128 + 64 * h : 192 + 64 * h, :] = halves(full)
    for k, copies in enumerate(waits):
        for copy in copies:
            copy.wait()
        for lo in range(k * chunk, k * chunk + chunk, sub):
            xs = x[lo : lo + sub, :]
            both = bdot(mq[...], xs, NT)
            weights = all_weights(both[:128] + both[128:])
            total = weights[:, :128]
            for tile in range(1, sub // 128):
                total = total + weights[:, 128 * tile : 128 * tile + 128]
            nacc[...] += total
            weights_b = weights.astype(BF16)
            ab_ref[:, :256] += bdot(weights_b, xs)
            ab_ref[:, 256:] += bdot(weights_b, u[lo : lo + sub, :])
    for h in range(2):
        feat = slice(32 * h, 32 * h + 32)
        rows = slice(64 * h, 64 * h + 64)
        pay[h, 0:32, 0:64] = edot(wfx[feat, :], ab_ref[rows, :256], NT)
        pay[h, 0:32, 64:128] = edot(wout[feat, :], ab_ref[rows, 256:], NT)
        norm = edot(jnp.ones((16, 128), BF16), nacc[rows, :], NT)[:8]
        pay[h, 32:40, 0:64] = norm
        pay[h, 32:40, 64:128] = norm
    mine_ref[...] = pay[me[1]]
    rest_ref[...] = pay[1 - me[1]]


def split3(value):
    high = value.astype(BF16)
    rest = value - high.astype(F32)
    mid = rest.astype(BF16)
    return [high, mid, (rest - mid.astype(F32)).astype(BF16)]


def token_kernel(me, sharp, pay, qkv, ws, wmid, wfx, wout, pack, attn_ref):
    head = me[1]
    feat = pl.ds(pl.multiple_of(32 * head, 32), 32)
    pack[0:32, :] = wfx[feat, :]
    pack[32:64, :] = wmid[feat, :]
    pack[64:96, :] = wout[feat, :]
    pack[96:128, 128:192] = ws[head]
    pack[96:128, 192:256] = jnp.zeros((32, 64), BF16)
    pack[128:144, :] = jnp.zeros((16, 256), BF16)
    root = 1.0 / math.sqrt(32.0)
    norm = pay[32:33, 0:64]
    token = pay[0:32, 0:64] / norm
    grad_so = pay[0:32, 64:128]
    maps = jnp.concatenate([qkv[head, 0], qkv[head, 1], qkv[head, 2]], axis=1)
    proj = fdot(maps, token, TN)
    query, key, value = proj[:32], proj[32:64], proj[64:]
    expo = jnp.exp(fdot(key, query, TN) * root)
    prob = expo / jnp.sum(expo, axis=0, keepdims=True)
    so = fdot(value, prob)
    grad_prob = fdot(value, grad_so, TN)
    grad_value = fdot(grad_so, prob, NT)
    grad_score = prob * (grad_prob - jnp.sum(prob * grad_prob, axis=0, keepdims=True)) * root
    grad_query = fdot(key, grad_score)
    grad_key = fdot(query, grad_score, NT)
    grads = jnp.concatenate([grad_query, grad_key, grad_value], axis=0)
    grad_token = fdot(maps, grads)
    grad_norm = -jnp.sum(grad_token * token, axis=0, keepdims=True) / norm
    inv = 1.0 / (jnp.zeros((1, 64), F32) + sharp[head])
    pack[96:128, 0:64] = so.astype(BF16)
    pack[96:128, 64:128] = (grad_token / norm).astype(BF16)
    parts = split3(grad_norm) + split3(inv) + [jnp.zeros((10, 64), BF16)]
    pack[128:144, 0:64] = jnp.concatenate(parts, axis=0)
    attn = fdot(token, grads, NT)
    for j in range(3):
        attn_ref[j] = attn[:, 32 * j : 32 * j + 32]


def centre(block):
    return block - jnp.mean(block, axis=0, keepdims=True)


def unpack_columns(parts):
    pick = lax.broadcasted_iota(jnp.int32, (16, 256), 0)
    lane = lax.broadcasted_iota(jnp.int32, (16, 256), 1)
    first = jnp.where(lane < 128, 0, 3)
    chosen = jnp.where((pick >= first) & (pick < first + 3), 1.0, 0.0).astype(BF16)
    cols = bdot(parts, chosen, TN)
    return cols[:, 128:], cols[:, :128] * cols[:, 128:]


def weight_kernel(
    scale, sub, unroll, me, own, other, ws, wmid, ab, mq, x, u, mine, rest,
    packs, grads, maps, mu, gn, gacc,
):
    points = x.shape[0]
    packs[me[1]] = own[...]
    packs[1 - me[1]] = other[...]
    maps[0:256, :] = mq[...]
    for h in range(2):
        rows = slice(64 * h, 64 * h + 64)
        pack = packs.at[h]
        inv, gn[rows, :] = unpack_columns(pack[128:144, 0:64])
        mu_h = centre(bdot(pack[96:128, 0:64], pack[64:96, :], TN)) * inv[:, :1]
        mx_h = centre(bdot(pack[96:128, 64:128], pack[0:32, :], TN)) * inv[:, :1]
        mu[rows, :] = mu_h.astype(BF16)
        maps[256 + 64 * h : 320 + 64 * h, :] = mx_h.astype(BF16)
    gacc[...] = jnp.zeros_like(gacc)

    def body(i, _):
        for j in range(unroll):
            here = pl.ds(pl.multiple_of((i * unroll + j) * sub, sub), sub)
            xs = x[here, :]
            both = bdot(maps[...], xs, NT)
            weights = all_weights(both[:128] + both[128:256])
            grad_w = both[256:] + bdot(mu[...], u[here, :], NT) + gn[:, :1]
            gacc[...] += bdot(all_logit_grads(weights, grad_w), xs)
        return 0

    lax.fori_loop(0, points // (sub * unroll), body, 0)
    for h in range(2):
        rows = slice(64 * h, 64 * h + 64)
        lo = 32 * h
        grads[lo : lo + 32, :] = edot(packs[h, 96:128, 64:128], ab[rows, :256])
        grads[64 + lo : 96 + lo, :] = scale * edot(ws[h], gacc[rows, :])
        grads[128 + lo : 160 + lo, :] = scale * edot(packs[h, 96:128, 0:64], ab[rows, 256:])
    score = scale * edot(wmid[...], gacc[...], NT)
    first = lax.broadcasted_iota(jnp.int32, (32, 128), 1) < 64
    score = jnp.where(first, score[:32], score[32:])
    grads[192:208, :128] = score[:16]
    grads[192:208, 128:] = score[16:]
    half = mine.shape[0]
    mine[...] = grads[pl.ds(pl.multiple_of(me[1] * half, 8), half), :]
    rest[...] = grads[pl.ds(pl.multiple_of((1 - me[1]) * half, 8), half), :]


def prepare_kernel(me, *refs):
    mq, mxu, gn, wcr, packs, parts, wide, tall = refs[8:]
    for g in range(4):
        packs[g, me[1]] = refs[g][...]
        packs[g, 1 - me[1]] = refs[4 + g][...]
        for h in range(2):
            at = 128 * g + 64 * h
            parts[:, at : at + 64] = packs[g, h, 128:144, 0:64]
    inv, columns = unpack_columns(parts[...])
    gn[...] = columns
    inv = inv[:, :1]
    for g in range(4):
        for h in range(2):
            pack = packs.at[g, h]
            at = 128 * g + 64 * h
            rows = slice(at, at + 64)
            score = bdot(pack[96:128, 128:192], pack[32:64, :], TN)
            from_x = bdot(pack[96:128, 64:128], pack[0:32, :], TN)
            wide[rows, :] = score
            wide[512 + at : 576 + at, :] = from_x
            from_u = bdot(pack[96:128, 0:64], pack[64:96, :], TN)
            mq[rows, :] = (score * (LOG2E * inv[rows])).astype(BF16)
            mxu[rows, :256] = (centre(from_x) * inv[rows]).astype(BF16)
            mxu[rows, 256:] = (centre(from_u) * inv[rows]).astype(BF16)
    half = pl.multiple_of(lax.div(me[0], 2) * 128, 128)
    tall[...] = wide[:, pl.ds(half, 128)].T
    wcr[...] = tall[pl.ds(pl.multiple_of(lax.rem(me[0], 2) * 64, 64), 64), :].astype(BF16)


def input_kernel(
    chunk, sub, mq, mxu, gn, wcr, x_hbm, u_hbm, grad,
    xu, out, logits, grad_w, pair, sems, out_sems,
):
    points = xu.shape[0]

    def project(slot, at):
        logits[slot] = bdot(mq[...], xu[pl.ds(at, sub), :256], NT)
        grad_w[slot] = bdot(mxu[...], xu[pl.ds(at, sub), :], NT)

    def derive(slot, at):
        for rows, cols in tiles(8, sub, 128):
            weights = slice_weights(logits[slot, rows, cols])
            full = grad_w[slot, rows, cols] + gn[rows, :]
            pair[slot, rows, cols] = logit_grad(weights, full)
            pair[slot, 512 + rows.start : 576 + rows.start, cols] = weights.astype(BF16)

    def emit(slot, at):
        out[:, pl.ds(at, sub)] = bdot(wcr[...], pair[slot]).astype(BF16)

    def sent(i):
        cols = pl.ds(pl.multiple_of(i * chunk, chunk), chunk)
        return pltpu.make_async_copy(out.at[:, cols], grad.at[:, cols], out_sems.at[i])

    start, wait = row_copies(x_hbm, u_hbm, xu, sems, chunk)
    count, per = points // chunk, chunk // sub
    for i in range(2):
        start(i)

    def body(i, _):
        wait(i)

        @pl.when(i + 2 < count)
        def _():
            start(i + 2)

        for part in range(per):
            at = pl.multiple_of(i * chunk + part * sub, sub)
            before = pl.multiple_of(jnp.maximum(at - sub, 0), sub)
            derive((part + 1) % 2, before)
            project(part % 2, at)
            emit((part + 1) % 2, before)

        @pl.when(i > 0)
        def _():
            sent(i - 1).start()

        return 0

    lax.fori_loop(0, count, body, 0)
    derive(1, points - sub)
    emit(1, points - sub)
    sent(count - 1).start()
    for i in range(count):
        sent(i).wait()


def final_kernel(me, half, other, attn_own, attn_other, fx, mid, out, score, attn, grads):
    rows = half.shape[0]
    grads[pl.ds(pl.multiple_of(me[1] * rows, 8), rows), :] = half[...]
    grads[pl.ds(pl.multiple_of((1 - me[1]) * rows, 8), rows), :] = other[...]
    attn[me[1]] = attn_own[...]
    attn[1 - me[1]] = attn_other[...]
    fx[...] = grads[0:64, :]
    mid[...] = grads[64:128, :]
    out[...] = grads[128:192, :]
    for h in range(2):
        for j in range(2):
            score[h, 16 * j : 16 * j + 16, :] = grads[
                192:208, 128 * j + 64 * h : 128 * j + 64 * h + 64
            ]


def shape(*dims, kind=F32):
    return jax.ShapeDtypeStruct(dims, kind)


def call(kernel, name, in_specs, out_shape, scratch, args, out_specs=None, flops=None):
    cost = None
    if flops is not None:
        cost = pl.CostEstimate(flops=flops, bytes_accessed=1 << 23, transcendentals=0)
    return pl.pallas_call(
        kernel,
        in_specs=in_specs,
        out_specs=out_specs if out_specs is not None else [VM] * len(out_shape),
        out_shape=out_shape,
        scratch_shapes=scratch,
        compiler_params=PARAMS,
        cost_estimate=cost,
        name=name,
    )(*args)


def first_pass(me, sharp, x, u, wmid, ws, wfx, wout, chunk=2048, sub=256):
    points = x.shape[0]

    def kernel(*refs):
        pool_kernel(chunk, sub, *refs)

    return call(
        kernel,
        "pool_pass",
        [SMEM, SMEM, HB, HB, VM, VM, VM, VM],
        [shape(40, 128), shape(40, 128), shape(128, 512), shape(256, 256, kind=BF16)]
        + [shape(points, 256, kind=BF16)] * 2,
        [
            pltpu.VMEM((2, 40, 128), F32),
            pltpu.VMEM((128, 128), F32),
            pltpu.SemaphoreType.DMA((2, points // chunk)),
        ],
        (me, sharp, x, u, wmid, ws, wfx, wout),
        flops=1 << 33,
    )


def token_pass(me, sharp, pay, qkv, ws, wmid, wfx, wout):
    return call(
        token_kernel,
        "token_pass",
        [SMEM, SMEM] + [VM] * 6,
        [shape(*PACK, kind=BF16), shape(3, 32, 32)],
        [],
        (me, sharp, pay, qkv, ws, wmid, wfx, wout),
    )


def weight_pass(me, scale, own, other, ws, wmid, ab, mq, x, u, sub=512, unroll=8):
    def kernel(*refs):
        weight_kernel(scale, sub, unroll, *refs)

    return call(
        kernel,
        "weight_pass",
        [SMEM] + [VM] * 8,
        [shape(104, 256)] * 2,
        [
            pltpu.VMEM((2,) + PACK, BF16),
            pltpu.VMEM((208, 256), F32),
            pltpu.VMEM((384, 256), BF16),
            pltpu.VMEM((128, 256), BF16),
            pltpu.VMEM((128, 128), F32),
            pltpu.VMEM((128, 256), F32),
        ],
        (me, own, other, ws, wmid, ab, mq, x, u),
        flops=1 << 33,
    )


def prepare(me, packs, others):
    return call(
        prepare_kernel,
        "prepare",
        [SMEM] + [VM] * 8,
        [
            shape(512, 256, kind=BF16),
            shape(512, 512, kind=BF16),
            shape(512, 128),
            shape(64, 1024, kind=BF16),
        ],
        [
            pltpu.VMEM((4, 2) + PACK, BF16),
            pltpu.VMEM((16, 512), BF16),
            pltpu.VMEM((1024, 256), F32),
            pltpu.VMEM((128, 1024), F32),
        ],
        (me, *packs, *others),
        flops=1 << 31,
    )


def input_pass(maps, x, u, chunk=2048, sub=256):
    points = x.shape[0]

    def kernel(*refs):
        input_kernel(chunk, sub, *refs)

    return call(
        kernel,
        "input_pass",
        [VM] * 4 + [HB] * 2,
        shape(64, points, kind=BF16),
        [
            pltpu.VMEM((points, 512), BF16),
            pltpu.VMEM((64, points), BF16),
            pltpu.VMEM((2, 512, sub), F32),
            pltpu.VMEM((2, 512, sub), F32),
            pltpu.VMEM((2, 1024, sub), BF16),
            pltpu.SemaphoreType.DMA((2, points // chunk)),
            pltpu.SemaphoreType.DMA((points // chunk,)),
        ],
        (*maps, x, u),
        out_specs=HB,
        flops=1 << 33,
    )


def final_pass(me, half, other, attn, attn_other):
    return call(
        final_kernel,
        "final_pass",
        [SMEM] + [VM] * 4,
        [shape(64, 256)] * 3 + [shape(2, 32, 64), shape(2, 3, 32, 32)],
        [pltpu.VMEM((208, 256), F32)],
        (me, half, other, attn, attn_other),
    )


def core_swap(value):
    return lax.ppermute(value, "core", [(0, 1), (1, 0)])


def y_sum(value):
    parts = [
        lax.ppermute(value, "y", [(i, i ^ k) for i in range(4)]).astype(F32) for k in range(1, 4)
    ]
    return (value.astype(F32) + parts[0]) + (parts[1] + parts[2])


def z_sum(value, beside=None):
    sent = jnp.broadcast_to(value[None], (8,) + value.shape)
    got = lax.all_to_all(sent, "z", 0, 0)
    if beside is not None:
        got, _ = lax.optimization_barrier((got, beside))
    got = got.astype(F32)
    total = got[0]
    for part in range(1, 8):
        total = total + got[part]
    return total


def shifted(value, k):
    return lax.ppermute(value, "head", [(i, (i + k) % 4) for i in range(4)])


def per_device(x, u, wfx, wmid, ws, sharp, qkv, wout):
    points = x.shape[0]
    scale = 1.0 / math.sqrt(points * 64)
    me = jnp.stack([lax.axis_index("head"), lax.axis_index("core")]).astype(jnp.int32)
    wfx = wfx.T
    wmid = wmid.T
    held = [
        pltpu.with_memory_space_constraint(v, pltpu.HBM) for v in (sharp, x, u, wmid, ws, wfx, wout)
    ]
    mine, rest, ab, mq, x, u = first_pass(me, *held)
    pay = z_sum(y_sum(mine + core_swap(rest)))
    pack, attn = token_pass(me, sharp, pay, qkv, ws, wmid, wfx, wout)
    other = core_swap(pack)
    attn_other = core_swap(attn)
    packs = [shifted(pack, k) for k in (1, 2, 3)]
    mine, rest = weight_pass(me, scale, pack, other, ws, wmid, ab, mq, x, u)
    mine, rest, packs, attn_other = lax.optimization_barrier((mine, rest, packs, attn_other))
    half = (mine + core_swap(rest)).astype(BF16)
    others = [core_swap(p) for p in packs]
    half = y_sum(half).astype(BF16)
    maps = prepare(me, [pack] + packs, [other] + others)
    half, maps = lax.optimization_barrier((half, maps))
    grad = input_pass(maps, held[1], held[2])
    half = z_sum(half, grad)
    fx, mid, out, score, attn = final_pass(me, half, core_swap(half), attn, attn_other)
    return grad.T, fx.T, mid.T, score, attn, out


def solution(mesh):
    fine = Mesh(np.asarray(mesh.devices).reshape(4, 8, 2, 4), PTS + ("head",))
    in_specs = (
        P(PTS, None),
        P(PTS, None),
        P(None, "head"),
        P(None, "head"),
        P("head", None, None),
        P("head"),
        P("head", None, None, None),
        P("head", None),
    )
    out_specs = (
        P(PTS, "head"),
        P(None, "head"),
        P(None, "head"),
        P("head", None, None),
        P("head", None, None, None),
        P("head", None),
    )
    return jax.shard_map(
        per_device, mesh=fine, in_specs=in_specs, out_specs=out_specs, check_vma=False
    )
```

```python
import math

import jax
import jax.numpy as jnp
import numpy as np
from jax import lax
from jax.experimental import pallas as pl
from jax.experimental.pallas import tpu as pltpu
from jax.sharding import Mesh
from jax.sharding import PartitionSpec as P

F32 = jnp.float32
BF16 = jnp.bfloat16
LOG2E = 1.4426950408889634
PTS = ("y", "z", "core")
NN = (((1,), (0,)), ((), ()))
NT = (((1,), (1,)), ((), ()))
TN = (((0,), (0,)), ((), ()))
SMEM = pl.BlockSpec(memory_space=pltpu.SMEM)
VM = pl.BlockSpec(memory_space=pltpu.VMEM)
HB = pl.BlockSpec(memory_space=pltpu.HBM)
PARAMS = pltpu.CompilerParams(vmem_limit_bytes=24 * 1024 * 1024)
PACK = (144, 256)
EARLY = 1024


def bdot(left, right, dims=NN):
    return lax.dot_general(left, right, dims, preferred_element_type=F32)


def halves(value):
    high = value.astype(BF16)
    return high, (value - high.astype(F32)).astype(BF16)


def edot(exact, value, dims=NN):
    high, low = halves(value)
    return bdot(exact, high, dims) + bdot(exact, low, dims)


def fdot(left, right, dims=NN):
    left_high, left_low = halves(left)
    right_high, right_low = halves(right)
    return (bdot(left_high, right_low, dims) + bdot(left_low, right_high, dims)) + bdot(
        left_high, right_high, dims
    )


def slice_weights(logits):
    expo = jnp.exp2(logits)
    return expo * (1.0 / jnp.sum(expo, axis=0, keepdims=True))


def all_weights(logits):
    rows, cols = logits.shape
    expo = jnp.exp2(logits).reshape(rows // 64, 64, cols)
    weights = expo * (1.0 / jnp.sum(expo, axis=1, keepdims=True))
    return weights.reshape(rows, cols)


def all_logit_grads(weights, grad_w):
    rows, cols = weights.shape
    weights = weights.reshape(rows // 64, 64, cols)
    prod = weights * grad_w.reshape(rows // 64, 64, cols)
    grad = prod - weights * jnp.sum(prod, axis=1, keepdims=True)
    return grad.reshape(rows, cols).astype(BF16)


def logit_grad(weights, grad_w):
    mean = jnp.sum(weights * grad_w, axis=0, keepdims=True)
    return (weights * (grad_w - mean)).astype(BF16)


def tiles(heads, cols, width):
    for h in range(heads):
        for lo in range(0, cols, width):
            yield slice(64 * h, 64 * h + 64), slice(lo, lo + width)


def pool_kernel(
    chunk, sub, me, sharp, x_hbm, u_hbm, wmid, ws, wfx, wout,
    mine_ref, rest_ref, ab_ref, mq, x, u, pay, nacc, sems,
):
    waits = []
    for k, lo in enumerate(range(0, x.shape[0], chunk)):
        copies = [
            pltpu.make_async_copy(src.at[lo : lo + chunk, :], dst.at[lo : lo + chunk, :], sems.at[j, k])
            for j, (src, dst) in enumerate(((x_hbm, x), (u_hbm, u)))
        ]
        for copy in copies:
            copy.start()
        waits.append(copies)
    ab_ref[...] = jnp.zeros_like(ab_ref)
    nacc[...] = jnp.zeros_like(nacc)
    for h in range(2):
        full = bdot(ws[h], wmid[32 * h : 32 * h + 32, :], TN) * (LOG2E / sharp[h])
        mq[64 * h : 64 * h + 64, :], mq[128 + 64 * h : 192 + 64 * h, :] = halves(full)
    for k, copies in enumerate(waits):
        for copy in copies:
            copy.wait()
        for lo in range(k * chunk, k * chunk + chunk, sub):
            xs = x[lo : lo + sub, :]
            both = bdot(mq[...], xs, NT)
            weights = all_weights(both[:128] + both[128:])
            total = weights[:, :128]
            for tile in range(1, sub // 128):
                total = total + weights[:, 128 * tile : 128 * tile + 128]
            nacc[...] += total
            weights_b = weights.astype(BF16)
            ab_ref[:, :256] += bdot(weights_b, xs)
            ab_ref[:, 256:] += bdot(weights_b, u[lo : lo + sub, :])
    for h in range(2):
        feat = slice(32 * h, 32 * h + 32)
        rows = slice(64 * h, 64 * h + 64)
        pay[h, 0:32, 0:64] = edot(wfx[feat, :], ab_ref[rows, :256], NT)
        pay[h, 0:32, 64:128] = edot(wout[feat, :], ab_ref[rows, 256:], NT)
        norm = edot(jnp.ones((16, 128), BF16), nacc[rows, :], NT)[:8]
        pay[h, 32:40, 0:64] = norm
        pay[h, 32:40, 64:128] = norm
    mine_ref[...] = pay[me[1]]
    rest_ref[...] = pay[1 - me[1]]


def split3(value):
    high = value.astype(BF16)
    rest = value - high.astype(F32)
    mid = rest.astype(BF16)
    return [high, mid, (rest - mid.astype(F32)).astype(BF16)]


def token_kernel(me, sharp, pay, qkv, ws, wmid, wfx, wout, pack, attn_ref):
    head = me[1]
    feat = pl.ds(pl.multiple_of(32 * head, 32), 32)
    pack[0:32, :] = wfx[feat, :]
    pack[32:64, :] = wmid[feat, :]
    pack[64:96, :] = wout[feat, :]
    pack[96:128, 128:192] = ws[head]
    pack[96:128, 192:256] = jnp.zeros((32, 64), BF16)
    pack[128:144, :] = jnp.zeros((16, 256), BF16)
    root = 1.0 / math.sqrt(32.0)
    norm = pay[32:33, 0:64]
    token = pay[0:32, 0:64] / norm
    grad_so = pay[0:32, 64:128]
    maps = jnp.concatenate([qkv[head, 0], qkv[head, 1], qkv[head, 2]], axis=1)
    proj = fdot(maps, token, TN)
    query, key, value = proj[:32], proj[32:64], proj[64:]
    expo = jnp.exp(fdot(key, query, TN) * root)
    prob = expo / jnp.sum(expo, axis=0, keepdims=True)
    so = fdot(value, prob)
    grad_prob = fdot(value, grad_so, TN)
    grad_value = fdot(grad_so, prob, NT)
    grad_score = prob * (grad_prob - jnp.sum(prob * grad_prob, axis=0, keepdims=True)) * root
    grad_query = fdot(key, grad_score)
    grad_key = fdot(query, grad_score, NT)
    grads = jnp.concatenate([grad_query, grad_key, grad_value], axis=0)
    grad_token = fdot(maps, grads)
    grad_norm = -jnp.sum(grad_token * token, axis=0, keepdims=True) / norm
    inv = 1.0 / (jnp.zeros((1, 64), F32) + sharp[head])
    pack[96:128, 0:64] = so.astype(BF16)
    pack[96:128, 64:128] = (grad_token / norm).astype(BF16)
    parts = split3(grad_norm) + split3(inv) + [jnp.zeros((10, 64), BF16)]
    pack[128:144, 0:64] = jnp.concatenate(parts, axis=0)
    attn = fdot(token, grads, NT)
    for j in range(3):
        attn_ref[j] = attn[:, 32 * j : 32 * j + 32]


def centre(block):
    return block - jnp.mean(block, axis=0, keepdims=True)


def unpack_columns(parts):
    pick = lax.broadcasted_iota(jnp.int32, (16, 256), 0)
    lane = lax.broadcasted_iota(jnp.int32, (16, 256), 1)
    first = jnp.where(lane < 128, 0, 3)
    chosen = jnp.where((pick >= first) & (pick < first + 3), 1.0, 0.0).astype(BF16)
    cols = bdot(parts, chosen, TN)
    return cols[:, 128:], cols[:, :128] * cols[:, 128:]


def weight_kernel(
    scale, sub, unroll, me, own, other, ws, wmid, ab, mq, x, u, mine, rest,
    packs, grads, maps, mu, gn, gacc,
):
    points = x.shape[0]
    packs[me[1]] = own[...]
    packs[1 - me[1]] = other[...]
    maps[0:256, :] = mq[...]
    for h in range(2):
        rows = slice(64 * h, 64 * h + 64)
        pack = packs.at[h]
        inv, gn[rows, :] = unpack_columns(pack[128:144, 0:64])
        mu_h = centre(bdot(pack[96:128, 0:64], pack[64:96, :], TN)) * inv[:, :1]
        mx_h = centre(bdot(pack[96:128, 64:128], pack[0:32, :], TN)) * inv[:, :1]
        mu[rows, :] = mu_h.astype(BF16)
        maps[256 + 64 * h : 320 + 64 * h, :] = mx_h.astype(BF16)
    gacc[...] = jnp.zeros_like(gacc)

    def body(i, _):
        for j in range(unroll):
            here = pl.ds(pl.multiple_of((i * unroll + j) * sub, sub), sub)
            xs = x[here, :]
            both = bdot(maps[...], xs, NT)
            weights = all_weights(both[:128] + both[128:256])
            grad_w = both[256:] + bdot(mu[...], u[here, :], NT) + gn[:, :1]
            gacc[...] += bdot(all_logit_grads(weights, grad_w), xs)
        return 0

    lax.fori_loop(0, points // (sub * unroll), body, 0)
    for h in range(2):
        rows = slice(64 * h, 64 * h + 64)
        lo = 32 * h
        grads[lo : lo + 32, :] = edot(packs[h, 96:128, 64:128], ab[rows, :256])
        grads[64 + lo : 96 + lo, :] = scale * edot(ws[h], gacc[rows, :])
        grads[128 + lo : 160 + lo, :] = scale * edot(packs[h, 96:128, 0:64], ab[rows, 256:])
    score = scale * edot(wmid[...], gacc[...], NT)
    first = lax.broadcasted_iota(jnp.int32, (32, 128), 1) < 64
    score = jnp.where(first, score[:32], score[32:])
    grads[192:208, :128] = score[:16]
    grads[192:208, 128:] = score[16:]
    half = mine.shape[0]
    mine[...] = grads[pl.ds(pl.multiple_of(me[1] * half, 8), half), :]
    rest[...] = grads[pl.ds(pl.multiple_of((1 - me[1]) * half, 8), half), :]


def prepare_kernel(me, *refs):
    mq, mxu, gn, wcr, packs, parts, wide, tall = refs[8:]
    for g in range(4):
        packs[g, me[1]] = refs[g][...]
        packs[g, 1 - me[1]] = refs[4 + g][...]
        for h in range(2):
            at = 128 * g + 64 * h
            parts[:, at : at + 64] = packs[g, h, 128:144, 0:64]
    inv, columns = unpack_columns(parts[...])
    gn[...] = columns
    inv = inv[:, :1]
    for g in range(4):
        for h in range(2):
            pack = packs.at[g, h]
            at = 128 * g + 64 * h
            rows = slice(at, at + 64)
            score = bdot(pack[96:128, 128:192], pack[32:64, :], TN)
            from_x = bdot(pack[96:128, 64:128], pack[0:32, :], TN)
            wide[rows, :] = score
            wide[512 + at : 576 + at, :] = from_x
            from_u = bdot(pack[96:128, 0:64], pack[64:96, :], TN)
            mq[rows, :] = (score * (LOG2E * inv[rows])).astype(BF16)
            mxu[rows, :256] = (centre(from_x) * inv[rows]).astype(BF16)
            mxu[rows, 256:] = (centre(from_u) * inv[rows]).astype(BF16)
    half = pl.multiple_of(lax.div(me[0], 2) * 128, 128)
    tall[...] = wide[:, pl.ds(half, 128)].T
    wcr[...] = tall[pl.ds(pl.multiple_of(lax.rem(me[0], 2) * 64, 64), 64), :].astype(BF16)


def columns_stages(sub, mq, mxu, gn, wcr, x, u, out, logits, grad_w, pair):
    def project(slot, at):
        here = pl.ds(at, sub)
        xs = x[here, :]
        logits[slot] = bdot(mq[...], xs, NT)
        grad_w[slot] = bdot(mxu[:, :256], xs, NT) + bdot(mxu[:, 256:], u[here, :], NT)

    def derive(slot):
        for rows, cols in tiles(8, sub, 256):
            weights = slice_weights(logits[slot, rows, cols])
            full = grad_w[slot, rows, cols] + gn[rows, :1]
            pair[slot, rows, cols] = logit_grad(weights, full)
            pair[slot, 512 + rows.start : 576 + rows.start, cols] = weights.astype(BF16)

    def emit(slot, at):
        out[:, pl.ds(at, sub)] = bdot(wcr[...], pair[slot]).astype(BF16)

    return project, derive, emit


def early_kernel(sub, mq, mxu, gn, wcr, x, u, grad, out, logits, grad_w, pair, sem):
    points = out.shape[1]
    project, derive, emit = columns_stages(
        sub, mq, mxu, gn, wcr, x, u, out, logits, grad_w, pair
    )
    for n in range(points // sub + 1):
        if n > 0:
            derive((n + 1) % 2)
        if n < points // sub:
            project(n % 2, n * sub)
        if n > 0:
            emit((n + 1) % 2, (n - 1) * sub)
    copy = pltpu.make_async_copy(out, grad.at[:, 0:points], sem)
    copy.start()
    copy.wait()


def late_kernel(
    cuts, sub, skip, mq, mxu, gn, wcr, x_hbm, u_hbm, begun, grad,
    x, u, out, logits, grad_w, pair, sems, out_sems,
):
    project, derive, emit = columns_stages(
        sub, mq, mxu, gn, wcr, x, u, out, logits, grad_w, pair
    )
    loads, stores = [], []
    for k, (lo, hi) in enumerate(cuts):
        loads.append(
            [
                pltpu.make_async_copy(
                    src.at[skip + lo : skip + hi, :], dst.at[lo:hi, :], sems.at[j, k]
                )
                for j, (src, dst) in enumerate(((x_hbm, x), (u_hbm, u)))
            ]
        )
        stores.append(
            pltpu.make_async_copy(out.at[:, lo:hi], grad.at[:, skip + lo : skip + hi], out_sems.at[k])
        )
    for copies in loads[:2]:
        for copy in copies:
            copy.start()
    for k, (lo, hi) in enumerate(cuts):
        for copy in loads[k]:
            copy.wait()
        if k + 2 < len(cuts):
            for copy in loads[k + 2]:
                copy.start()
        for at in range(lo, hi, sub):
            slot = (at // sub) % 2
            if at > 0:
                derive(1 - slot)
            project(slot, at)
            if at > 0:
                emit(1 - slot, at - sub)
        if k > 0:
            stores[k - 1].start()
    slot = (cuts[-1][1] // sub - 1) % 2
    derive(slot)
    emit(slot, cuts[-1][1] - sub)
    stores[-1].start()
    for store in stores:
        store.wait()


def final_kernel(me, half, other, attn_own, attn_other, fx, mid, out, score, attn, grads):
    rows = half.shape[0]
    grads[pl.ds(pl.multiple_of(me[1] * rows, 8), rows), :] = half[...]
    grads[pl.ds(pl.multiple_of((1 - me[1]) * rows, 8), rows), :] = other[...]
    attn[me[1]] = attn_own[...]
    attn[1 - me[1]] = attn_other[...]
    fx[...] = grads[0:64, :]
    mid[...] = grads[64:128, :]
    out[...] = grads[128:192, :]
    for h in range(2):
        for j in range(2):
            score[h, 16 * j : 16 * j + 16, :] = grads[
                192:208, 128 * j + 64 * h : 128 * j + 64 * h + 64
            ]


def shape(*dims, kind=F32):
    return jax.ShapeDtypeStruct(dims, kind)


def call(
    kernel, name, in_specs, out_shape, scratch, args, out_specs=None, flops=None, aliases=None
):
    cost = None
    if flops is not None:
        cost = pl.CostEstimate(flops=flops, bytes_accessed=1 << 23, transcendentals=0)
    return pl.pallas_call(
        kernel,
        in_specs=in_specs,
        out_specs=out_specs if out_specs is not None else [VM] * len(out_shape),
        out_shape=out_shape,
        scratch_shapes=scratch,
        compiler_params=PARAMS,
        cost_estimate=cost,
        input_output_aliases=aliases or {},
        name=name,
    )(*args)


def first_pass(me, sharp, x, u, wmid, ws, wfx, wout, chunk=2048, sub=256):
    points = x.shape[0]

    def kernel(*refs):
        pool_kernel(chunk, sub, *refs)

    return call(
        kernel,
        "pool_pass",
        [SMEM, SMEM, HB, HB, VM, VM, VM, VM],
        [shape(40, 128), shape(40, 128), shape(128, 512), shape(256, 256, kind=BF16)]
        + [shape(points, 256, kind=BF16)] * 2,
        [
            pltpu.VMEM((2, 40, 128), F32),
            pltpu.VMEM((128, 128), F32),
            pltpu.SemaphoreType.DMA((2, points // chunk)),
        ],
        (me, sharp, x, u, wmid, ws, wfx, wout),
        flops=1 << 33,
    )


def token_pass(me, sharp, pay, qkv, ws, wmid, wfx, wout):
    return call(
        token_kernel,
        "token_pass",
        [SMEM, SMEM] + [VM] * 6,
        [shape(*PACK, kind=BF16), shape(3, 32, 32)],
        [],
        (me, sharp, pay, qkv, ws, wmid, wfx, wout),
    )


def weight_pass(me, scale, own, other, ws, wmid, ab, mq, x, u, sub=512, unroll=8):
    def kernel(*refs):
        weight_kernel(scale, sub, unroll, *refs)

    return call(
        kernel,
        "weight_pass",
        [SMEM] + [VM] * 8,
        [shape(104, 256)] * 2,
        [
            pltpu.VMEM((2,) + PACK, BF16),
            pltpu.VMEM((208, 256), F32),
            pltpu.VMEM((384, 256), BF16),
            pltpu.VMEM((128, 256), BF16),
            pltpu.VMEM((128, 128), F32),
            pltpu.VMEM((128, 256), F32),
        ],
        (me, own, other, ws, wmid, ab, mq, x, u),
        flops=1 << 33,
    )


def prepare(me, packs, others):
    return call(
        prepare_kernel,
        "prepare",
        [SMEM] + [VM] * 8,
        [
            shape(512, 256, kind=BF16),
            shape(512, 512, kind=BF16),
            shape(512, 128),
            shape(64, 1024, kind=BF16),
        ],
        [
            pltpu.VMEM((4, 2) + PACK, BF16),
            pltpu.VMEM((16, 512), BF16),
            pltpu.VMEM((1024, 256), F32),
            pltpu.VMEM((128, 1024), F32),
        ],
        (me, *packs, *others),
        flops=1 << 31,
    )


def stage_scratch(points, sub):
    return [
        pltpu.VMEM((64, points), BF16),
        pltpu.VMEM((2, 512, sub), F32),
        pltpu.VMEM((2, 512, sub), F32),
        pltpu.VMEM((2, 1024, sub), BF16),
    ]


def early_pass(maps, x, u, points, sub=256):
    def kernel(*refs):
        early_kernel(sub, *refs)

    return call(
        kernel,
        "early_pass",
        [VM] * 6,
        shape(64, x.shape[0], kind=BF16),
        stage_scratch(points, sub) + [pltpu.SemaphoreType.DMA],
        (*maps, x, u),
        out_specs=HB,
        flops=1 << 32,
    )


def late_pass(maps, x, u, begun, skip, chunk=2048, sub=256):
    points = x.shape[0] - skip
    marks = list(range(points, 0, -chunk))[::-1]
    cuts = list(zip([0] + marks[:-1], marks))

    def kernel(*refs):
        late_kernel(cuts, sub, skip, *refs)

    return call(
        kernel,
        "late_pass",
        [VM] * 4 + [HB] * 3,
        shape(64, x.shape[0], kind=BF16),
        [pltpu.VMEM((points, 256), BF16)] * 2
        + stage_scratch(points, sub)
        + [
            pltpu.SemaphoreType.DMA((2, len(cuts))),
            pltpu.SemaphoreType.DMA((len(cuts),)),
        ],
        (*maps, x, u, begun),
        out_specs=HB,
        flops=1 << 33,
        aliases={6: 0},
    )


def final_pass(me, half, other, attn, attn_other):
    return call(
        final_kernel,
        "final_pass",
        [SMEM] + [VM] * 4,
        [shape(64, 256)] * 3 + [shape(2, 32, 64), shape(2, 3, 32, 32)],
        [pltpu.VMEM((208, 256), F32)],
        (me, half, other, attn, attn_other),
    )


def core_swap(value):
    return lax.ppermute(value, "core", [(0, 1), (1, 0)])


def y_sum(value):
    parts = [
        lax.ppermute(value, "y", [(i, i ^ k) for i in range(4)]).astype(F32) for k in range(1, 4)
    ]
    return (value.astype(F32) + parts[0]) + (parts[1] + parts[2])


def z_sum(value, beside=None):
    sent = jnp.broadcast_to(value[None], (8,) + value.shape)
    got = lax.all_to_all(sent, "z", 0, 0)
    if beside is not None:
        got, _ = lax.optimization_barrier((got, beside))
    got = got.astype(F32)
    total = got[0]
    for part in range(1, 8):
        total = total + got[part]
    return total


def shifted(value, k):
    return lax.ppermute(value, "head", [(i, (i + k) % 4) for i in range(4)])


def per_device(x, u, wfx, wmid, ws, sharp, qkv, wout):
    points = x.shape[0]
    scale = 1.0 / math.sqrt(points * 64)
    me = jnp.stack([lax.axis_index("head"), lax.axis_index("core")]).astype(jnp.int32)
    wfx = wfx.T
    wmid = wmid.T
    held = [
        pltpu.with_memory_space_constraint(v, pltpu.HBM) for v in (sharp, x, u, wmid, ws, wfx, wout)
    ]
    mine, rest, ab, mq, x, u = first_pass(me, *held)
    pay = z_sum(y_sum(mine + core_swap(rest)))
    pack, attn = token_pass(me, sharp, pay, qkv, ws, wmid, wfx, wout)
    other = core_swap(pack)
    attn_other = core_swap(attn)
    packs = [shifted(pack, k) for k in (1, 2, 3)]
    mine, rest = weight_pass(me, scale, pack, other, ws, wmid, ab, mq, x, u)
    mine, rest, packs, attn_other = lax.optimization_barrier((mine, rest, packs, attn_other))
    half = (mine + core_swap(rest)).astype(BF16)
    others = [core_swap(p) for p in packs]
    half = y_sum(half).astype(BF16)
    maps = prepare(me, [pack] + packs, [other] + others)
    grad = early_pass(maps, x, u, EARLY)
    half, maps, grad = lax.optimization_barrier((half, maps, grad))
    grad = late_pass(maps, held[1], held[2], grad, EARLY)
    half = z_sum(half, grad)
    fx, mid, out, score, attn = final_pass(me, half, core_swap(half), attn, attn_other)
    return grad.T, fx.T, mid.T, score, attn, out


def solution(mesh):
    fine = Mesh(np.asarray(mesh.devices).reshape(4, 8, 2, 4), PTS + ("head",))
    in_specs = (
        P(PTS, None),
        P(PTS, None),
        P(None, "head"),
        P(None, "head"),
        P("head", None, None),
        P("head"),
        P("head", None, None, None),
        P("head", None),
    )
    out_specs = (
        P(PTS, "head"),
        P(None, "head"),
        P(None, "head"),
        P("head", None, None),
        P("head", None, None, None),
        P("head", None),
    )
    return jax.shard_map(
        per_device, mesh=fine, in_specs=in_specs, out_specs=out_specs, check_vma=False
    )
```

```python
import math

import jax
import jax.numpy as jnp
import numpy as np
from jax import lax
from jax.experimental import pallas as pl
from jax.experimental.pallas import tpu as pltpu
from jax.sharding import Mesh
from jax.sharding import PartitionSpec as P

F32 = jnp.float32
BF16 = jnp.bfloat16
LOG2E = 1.4426950408889634
PTS = ("y", "z", "core")
NN = (((1,), (0,)), ((), ()))
NT = (((1,), (1,)), ((), ()))
TN = (((0,), (0,)), ((), ()))
SMEM = pl.BlockSpec(memory_space=pltpu.SMEM)
VM = pl.BlockSpec(memory_space=pltpu.VMEM)
HB = pl.BlockSpec(memory_space=pltpu.HBM)
PARAMS = pltpu.CompilerParams(vmem_limit_bytes=24 * 1024 * 1024)
PACK = (144, 256)
EARLY = 512


def bdot(left, right, dims=NN):
    return lax.dot_general(left, right, dims, preferred_element_type=F32)


def halves(value):
    high = value.astype(BF16)
    return high, (value - high.astype(F32)).astype(BF16)


def edot(exact, value, dims=NN):
    high, low = halves(value)
    return bdot(exact, high, dims) + bdot(exact, low, dims)


def fdot(left, right, dims=NN):
    left_high, left_low = halves(left)
    right_high, right_low = halves(right)
    return (bdot(left_high, right_low, dims) + bdot(left_low, right_high, dims)) + bdot(
        left_high, right_high, dims
    )


def slice_weights(logits):
    expo = jnp.exp2(logits)
    return expo * (1.0 / jnp.sum(expo, axis=0, keepdims=True))


def all_weights(logits):
    rows, cols = logits.shape
    expo = jnp.exp2(logits).reshape(rows // 64, 64, cols)
    weights = expo * (1.0 / jnp.sum(expo, axis=1, keepdims=True))
    return weights.reshape(rows, cols)


def all_logit_grads(weights, grad_w):
    rows, cols = weights.shape
    weights = weights.reshape(rows // 64, 64, cols)
    prod = weights * grad_w.reshape(rows // 64, 64, cols)
    grad = prod - weights * jnp.sum(prod, axis=1, keepdims=True)
    return grad.reshape(rows, cols).astype(BF16)


def logit_grad(weights, grad_w):
    mean = jnp.sum(weights * grad_w, axis=0, keepdims=True)
    return (weights * (grad_w - mean)).astype(BF16)


def tiles(heads, cols, width):
    for h in range(heads):
        for lo in range(0, cols, width):
            yield slice(64 * h, 64 * h + 64), slice(lo, lo + width)


def pool_kernel(
    chunk, sub, me, sharp, x_hbm, u_hbm, wmid, ws, wfx, wout,
    mine_ref, rest_ref, ab_ref, mq, x, u, pay, nacc, sems,
):
    waits = []
    for k, lo in enumerate(range(0, x.shape[0], chunk)):
        copies = [
            pltpu.make_async_copy(src.at[lo : lo + chunk, :], dst.at[lo : lo + chunk, :], sems.at[j, k])
            for j, (src, dst) in enumerate(((x_hbm, x), (u_hbm, u)))
        ]
        for copy in copies:
            copy.start()
        waits.append(copies)
    ab_ref[...] = jnp.zeros_like(ab_ref)
    nacc[...] = jnp.zeros_like(nacc)
    for h in range(2):
        full = bdot(ws[h], wmid[32 * h : 32 * h + 32, :], TN) * (LOG2E / sharp[h])
        mq[64 * h : 64 * h + 64, :], mq[128 + 64 * h : 192 + 64 * h, :] = halves(full)
    for k, copies in enumerate(waits):
        for copy in copies:
            copy.wait()
        for lo in range(k * chunk, k * chunk + chunk, sub):
            xs = x[lo : lo + sub, :]
            both = bdot(mq[...], xs, NT)
            weights = all_weights(both[:128] + both[128:])
            total = weights[:, :128]
            for tile in range(1, sub // 128):
                total = total + weights[:, 128 * tile : 128 * tile + 128]
            nacc[...] += total
            weights_b = weights.astype(BF16)
            ab_ref[:, :256] += bdot(weights_b, xs)
            ab_ref[:, 256:] += bdot(weights_b, u[lo : lo + sub, :])
    for h in range(2):
        feat = slice(32 * h, 32 * h + 32)
        rows = slice(64 * h, 64 * h + 64)
        pay[h, 0:32, 0:64] = edot(wfx[feat, :], ab_ref[rows, :256], NT)
        pay[h, 0:32, 64:128] = edot(wout[feat, :], ab_ref[rows, 256:], NT)
        norm = edot(jnp.ones((16, 128), BF16), nacc[rows, :], NT)[:8]
        pay[h, 32:40, 0:64] = norm
        pay[h, 32:40, 64:128] = norm
    mine_ref[...] = pay[me[1]]
    rest_ref[...] = pay[1 - me[1]]


def split3(value):
    high = value.astype(BF16)
    rest = value - high.astype(F32)
    mid = rest.astype(BF16)
    return [high, mid, (rest - mid.astype(F32)).astype(BF16)]


def token_kernel(me, sharp, pay, qkv, ws, wmid, wfx, wout, pack, attn_ref):
    head = me[1]
    feat = pl.ds(pl.multiple_of(32 * head, 32), 32)
    pack[0:32, :] = wfx[feat, :]
    pack[32:64, :] = wmid[feat, :]
    pack[64:96, :] = wout[feat, :]
    pack[96:128, 128:192] = ws[head]
    pack[96:128, 192:256] = jnp.zeros((32, 64), BF16)
    pack[128:144, :] = jnp.zeros((16, 256), BF16)
    root = 1.0 / math.sqrt(32.0)
    norm = pay[32:33, 0:64]
    token = pay[0:32, 0:64] / norm
    grad_so = pay[0:32, 64:128]
    maps = jnp.concatenate([qkv[head, 0], qkv[head, 1], qkv[head, 2]], axis=1)
    proj = fdot(maps, token, TN)
    query, key, value = proj[:32], proj[32:64], proj[64:]
    expo = jnp.exp(fdot(key, query, TN) * root)
    prob = expo / jnp.sum(expo, axis=0, keepdims=True)
    so = fdot(value, prob)
    grad_prob = fdot(value, grad_so, TN)
    grad_value = fdot(grad_so, prob, NT)
    grad_score = prob * (grad_prob - jnp.sum(prob * grad_prob, axis=0, keepdims=True)) * root
    grad_query = fdot(key, grad_score)
    grad_key = fdot(query, grad_score, NT)
    grads = jnp.concatenate([grad_query, grad_key, grad_value], axis=0)
    grad_token = fdot(maps, grads)
    grad_norm = -jnp.sum(grad_token * token, axis=0, keepdims=True) / norm
    inv = 1.0 / (jnp.zeros((1, 64), F32) + sharp[head])
    pack[96:128, 0:64] = so.astype(BF16)
    pack[96:128, 64:128] = (grad_token / norm).astype(BF16)
    parts = split3(grad_norm) + split3(inv) + [jnp.zeros((10, 64), BF16)]
    pack[128:144, 0:64] = jnp.concatenate(parts, axis=0)
    attn = fdot(token, grads, NT)
    for j in range(3):
        attn_ref[j] = attn[:, 32 * j : 32 * j + 32]


def centre(block):
    return block - jnp.mean(block, axis=0, keepdims=True)


def unpack_columns(parts):
    pick = lax.broadcasted_iota(jnp.int32, (16, 256), 0)
    lane = lax.broadcasted_iota(jnp.int32, (16, 256), 1)
    first = jnp.where(lane < 128, 0, 3)
    chosen = jnp.where((pick >= first) & (pick < first + 3), 1.0, 0.0).astype(BF16)
    cols = bdot(parts, chosen, TN)
    return cols[:, 128:], cols[:, :128] * cols[:, 128:]


def weight_kernel(
    scale, sub, unroll, me, own, other, ws, wmid, ab, mq, x, u, mine, rest,
    packs, grads, maps, mu, gn, gacc,
):
    points = x.shape[0]
    packs[me[1]] = own[...]
    packs[1 - me[1]] = other[...]
    maps[0:256, :] = mq[...]
    for h in range(2):
        rows = slice(64 * h, 64 * h + 64)
        pack = packs.at[h]
        inv, gn[rows, :] = unpack_columns(pack[128:144, 0:64])
        mu_h = centre(bdot(pack[96:128, 0:64], pack[64:96, :], TN)) * inv[:, :1]
        mx_h = centre(bdot(pack[96:128, 64:128], pack[0:32, :], TN)) * inv[:, :1]
        mu[rows, :] = mu_h.astype(BF16)
        maps[256 + 64 * h : 320 + 64 * h, :] = mx_h.astype(BF16)
    gacc[...] = jnp.zeros_like(gacc)

    def body(i, _):
        for j in range(unroll):
            here = pl.ds(pl.multiple_of((i * unroll + j) * sub, sub), sub)
            xs = x[here, :]
            both = bdot(maps[...], xs, NT)
            weights = all_weights(both[:128] + both[128:256])
            grad_w = both[256:] + bdot(mu[...], u[here, :], NT) + gn[:, :1]
            gacc[...] += bdot(all_logit_grads(weights, grad_w), xs)
        return 0

    lax.fori_loop(0, points // (sub * unroll), body, 0)
    for h in range(2):
        rows = slice(64 * h, 64 * h + 64)
        lo = 32 * h
        grads[lo : lo + 32, :] = edot(packs[h, 96:128, 64:128], ab[rows, :256])
        grads[64 + lo : 96 + lo, :] = scale * edot(ws[h], gacc[rows, :])
        grads[128 + lo : 160 + lo, :] = scale * edot(packs[h, 96:128, 0:64], ab[rows, 256:])
    score = scale * edot(wmid[...], gacc[...], NT)
    first = lax.broadcasted_iota(jnp.int32, (32, 128), 1) < 64
    score = jnp.where(first, score[:32], score[32:])
    grads[192:208, :128] = score[:16]
    grads[192:208, 128:] = score[16:]
    half = mine.shape[0]
    mine[...] = grads[pl.ds(pl.multiple_of(me[1] * half, 8), half), :]
    rest[...] = grads[pl.ds(pl.multiple_of((1 - me[1]) * half, 8), half), :]


def prepare_maps(me, refs, mq, mxu, gn, wcr, packs, parts, wide, tall):
    for g in range(4):
        packs[g, me[1]] = refs[g][...]
        packs[g, 1 - me[1]] = refs[4 + g][...]
        for h in range(2):
            at = 128 * g + 64 * h
            parts[:, at : at + 64] = packs[g, h, 128:144, 0:64]
    inv, columns = unpack_columns(parts[...])
    gn[...] = columns
    inv = inv[:, :1]
    for g in range(4):
        for h in range(2):
            pack = packs.at[g, h]
            at = 128 * g + 64 * h
            rows = slice(at, at + 64)
            score = bdot(pack[96:128, 128:192], pack[32:64, :], TN)
            from_x = bdot(pack[96:128, 64:128], pack[0:32, :], TN)
            wide[rows, :] = score
            wide[512 + at : 576 + at, :] = from_x
            from_u = bdot(pack[96:128, 0:64], pack[64:96, :], TN)
            mq[rows, :] = (score * (LOG2E * inv[rows])).astype(BF16)
            mxu[rows, :256] = (centre(from_x) * inv[rows]).astype(BF16)
            mxu[rows, 256:] = (centre(from_u) * inv[rows]).astype(BF16)
    half = pl.multiple_of(lax.div(me[0], 2) * 128, 128)
    tall[...] = wide[:, pl.ds(half, 128)].T
    wcr[...] = tall[pl.ds(pl.multiple_of(lax.rem(me[0], 2) * 64, 64), 64), :].astype(BF16)


def columns_stages(sub, mq, mxu, gn, wcr, x, u, out, logits, grad_w, pair):
    def project(slot, at):
        here = pl.ds(at, sub)
        xs = x[here, :]
        logits[slot] = bdot(mq[...], xs, NT)
        grad_w[slot] = bdot(mxu[:, :256], xs, NT) + bdot(mxu[:, 256:], u[here, :], NT)

    def derive(slot):
        for rows, cols in tiles(8, sub, 256):
            weights = slice_weights(logits[slot, rows, cols])
            full = grad_w[slot, rows, cols] + gn[rows, :1]
            pair[slot, rows, cols] = logit_grad(weights, full)
            pair[slot, 512 + rows.start : 576 + rows.start, cols] = weights.astype(BF16)

    def emit(slot, at):
        out[:, pl.ds(at, sub)] = bdot(wcr[...], pair[slot]).astype(BF16)

    return project, derive, emit


def early_kernel(sub, me, *refs):
    x, u, mq, mxu, gn, wcr, grad = refs[8:15]
    packs, parts, wide, tall, out, logits, grad_w, pair, sem = refs[15:]
    prepare_maps(me, refs[:8], mq, mxu, gn, wcr, packs, parts, wide, tall)
    points = out.shape[1]
    project, derive, emit = columns_stages(
        sub, mq, mxu, gn, wcr, x, u, out, logits, grad_w, pair
    )
    for n in range(points // sub + 1):
        if n > 0:
            derive((n + 1) % 2)
        if n < points // sub:
            project(n % 2, n * sub)
        if n > 0:
            emit((n + 1) % 2, (n - 1) * sub)
    copy = pltpu.make_async_copy(out, grad.at[:, 0:points], sem)
    copy.start()
    copy.wait()


def late_kernel(
    cuts, sub, skip, mq, mxu, gn, wcr, x_hbm, u_hbm, begun, grad,
    x, u, out, logits, grad_w, pair, sems, out_sems,
):
    project, derive, emit = columns_stages(
        sub, mq, mxu, gn, wcr, x, u, out, logits, grad_w, pair
    )
    loads, stores = [], []
    for k, (lo, hi) in enumerate(cuts):
        loads.append(
            [
                pltpu.make_async_copy(
                    src.at[skip + lo : skip + hi, :], dst.at[lo:hi, :], sems.at[j, k]
                )
                for j, (src, dst) in enumerate(((x_hbm, x), (u_hbm, u)))
            ]
        )
        stores.append(
            pltpu.make_async_copy(out.at[:, lo:hi], grad.at[:, skip + lo : skip + hi], out_sems.at[k])
        )
    for copies in loads[:2]:
        for copy in copies:
            copy.start()
    for k, (lo, hi) in enumerate(cuts):
        for copy in loads[k]:
            copy.wait()
        if k + 2 < len(cuts):
            for copy in loads[k + 2]:
                copy.start()
        for at in range(lo, hi, sub):
            slot = (at // sub) % 2
            if at > 0:
                derive(1 - slot)
            project(slot, at)
            if at > 0:
                emit(1 - slot, at - sub)
        if k > 0:
            stores[k - 1].start()
    slot = (cuts[-1][1] // sub - 1) % 2
    derive(slot)
    emit(slot, cuts[-1][1] - sub)
    stores[-1].start()
    for store in stores:
        store.wait()


def final_kernel(me, half, other, attn_own, attn_other, fx, mid, out, score, attn, grads):
    rows = half.shape[0]
    grads[pl.ds(pl.multiple_of(me[1] * rows, 8), rows), :] = half[...]
    grads[pl.ds(pl.multiple_of((1 - me[1]) * rows, 8), rows), :] = other[...]
    attn[me[1]] = attn_own[...]
    attn[1 - me[1]] = attn_other[...]
    fx[...] = grads[0:64, :]
    mid[...] = grads[64:128, :]
    out[...] = grads[128:192, :]
    for h in range(2):
        for j in range(2):
            score[h, 16 * j : 16 * j + 16, :] = grads[
                192:208, 128 * j + 64 * h : 128 * j + 64 * h + 64
            ]


def shape(*dims, kind=F32):
    return jax.ShapeDtypeStruct(dims, kind)


def call(
    kernel, name, in_specs, out_shape, scratch, args, out_specs=None, flops=None, aliases=None
):
    cost = None
    if flops is not None:
        cost = pl.CostEstimate(flops=flops, bytes_accessed=1 << 23, transcendentals=0)
    return pl.pallas_call(
        kernel,
        in_specs=in_specs,
        out_specs=out_specs if out_specs is not None else [VM] * len(out_shape),
        out_shape=out_shape,
        scratch_shapes=scratch,
        compiler_params=PARAMS,
        cost_estimate=cost,
        input_output_aliases=aliases or {},
        name=name,
    )(*args)


def first_pass(me, sharp, x, u, wmid, ws, wfx, wout, chunk=2048, sub=256):
    points = x.shape[0]

    def kernel(*refs):
        pool_kernel(chunk, sub, *refs)

    return call(
        kernel,
        "pool_pass",
        [SMEM, SMEM, HB, HB, VM, VM, VM, VM],
        [shape(40, 128), shape(40, 128), shape(128, 512), shape(256, 256, kind=BF16)]
        + [shape(points, 256, kind=BF16)] * 2,
        [
            pltpu.VMEM((2, 40, 128), F32),
            pltpu.VMEM((128, 128), F32),
            pltpu.SemaphoreType.DMA((2, points // chunk)),
        ],
        (me, sharp, x, u, wmid, ws, wfx, wout),
        flops=1 << 33,
    )


def token_pass(me, sharp, pay, qkv, ws, wmid, wfx, wout):
    return call(
        token_kernel,
        "token_pass",
        [SMEM, SMEM] + [VM] * 6,
        [shape(*PACK, kind=BF16), shape(3, 32, 32)],
        [],
        (me, sharp, pay, qkv, ws, wmid, wfx, wout),
    )


def weight_pass(me, scale, own, other, ws, wmid, ab, mq, x, u, sub=512, unroll=8):
    def kernel(*refs):
        weight_kernel(scale, sub, unroll, *refs)

    return call(
        kernel,
        "weight_pass",
        [SMEM] + [VM] * 8,
        [shape(104, 256)] * 2,
        [
            pltpu.VMEM((2,) + PACK, BF16),
            pltpu.VMEM((208, 256), F32),
            pltpu.VMEM((384, 256), BF16),
            pltpu.VMEM((128, 256), BF16),
            pltpu.VMEM((128, 128), F32),
            pltpu.VMEM((128, 256), F32),
        ],
        (me, own, other, ws, wmid, ab, mq, x, u),
        flops=1 << 33,
    )


def stage_scratch(points, sub):
    return [
        pltpu.VMEM((64, points), BF16),
        pltpu.VMEM((2, 512, sub), F32),
        pltpu.VMEM((2, 512, sub), F32),
        pltpu.VMEM((2, 1024, sub), BF16),
    ]


def early_pass(me, packs, others, x, u, points, sub=256):
    def kernel(*refs):
        early_kernel(sub, *refs)

    return call(
        kernel,
        "early_pass",
        [SMEM] + [VM] * 10,
        [
            shape(512, 256, kind=BF16),
            shape(512, 512, kind=BF16),
            shape(512, 128),
            shape(64, 1024, kind=BF16),
            shape(64, x.shape[0], kind=BF16),
        ],
        [
            pltpu.VMEM((4, 2) + PACK, BF16),
            pltpu.VMEM((16, 512), BF16),
            pltpu.VMEM((1024, 256), F32),
            pltpu.VMEM((128, 1024), F32),
        ]
        + stage_scratch(points, sub)
        + [pltpu.SemaphoreType.DMA],
        (me, *packs, *others, x, u),
        out_specs=[VM] * 4 + [HB],
        flops=1 << 32,
    )


def late_pass(maps, x, u, begun, skip, chunk=2048, sub=256):
    points = x.shape[0] - skip
    marks = list(range(points, 0, -chunk))[::-1]
    cuts = list(zip([0] + marks[:-1], marks))

    def kernel(*refs):
        late_kernel(cuts, sub, skip, *refs)

    return call(
        kernel,
        "late_pass",
        [VM] * 4 + [HB] * 3,
        shape(64, x.shape[0], kind=BF16),
        [pltpu.VMEM((points, 256), BF16)] * 2
        + stage_scratch(points, sub)
        + [
            pltpu.SemaphoreType.DMA((2, len(cuts))),
            pltpu.SemaphoreType.DMA((len(cuts),)),
        ],
        (*maps, x, u, begun),
        out_specs=HB,
        flops=1 << 33,
        aliases={6: 0},
    )


def final_pass(me, half, other, attn, attn_other):
    return call(
        final_kernel,
        "final_pass",
        [SMEM] + [VM] * 4,
        [shape(64, 256)] * 3 + [shape(2, 32, 64), shape(2, 3, 32, 32)],
        [pltpu.VMEM((208, 256), F32)],
        (me, half, other, attn, attn_other),
    )


def core_swap(value):
    return lax.ppermute(value, "core", [(0, 1), (1, 0)])


def y_sum(value):
    parts = [
        lax.ppermute(value, "y", [(i, i ^ k) for i in range(4)]).astype(F32) for k in range(1, 4)
    ]
    return (value.astype(F32) + parts[0]) + (parts[1] + parts[2])


def z_sum(value, beside=None):
    sent = jnp.broadcast_to(value[None], (8,) + value.shape)
    got = lax.all_to_all(sent, "z", 0, 0)
    if beside is not None:
        got, _ = lax.optimization_barrier((got, beside))
    got = got.astype(F32)
    total = got[0]
    for part in range(1, 8):
        total = total + got[part]
    return total


def shifted(value, k):
    return lax.ppermute(value, "head", [(i, (i + k) % 4) for i in range(4)])


def per_device(x, u, wfx, wmid, ws, sharp, qkv, wout):
    points = x.shape[0]
    scale = 1.0 / math.sqrt(points * 64)
    me = jnp.stack([lax.axis_index("head"), lax.axis_index("core")]).astype(jnp.int32)
    wfx = wfx.T
    wmid = wmid.T
    held = [
        pltpu.with_memory_space_constraint(v, pltpu.HBM) for v in (sharp, x, u, wmid, ws, wfx, wout)
    ]
    mine, rest, ab, mq, x, u = first_pass(me, *held)
    pay = z_sum(y_sum(mine + core_swap(rest)))
    pack, attn = token_pass(me, sharp, pay, qkv, ws, wmid, wfx, wout)
    other = core_swap(pack)
    attn_other = core_swap(attn)
    packs = [shifted(pack, k) for k in (1, 2, 3)]
    mine, rest = weight_pass(me, scale, pack, other, ws, wmid, ab, mq, x, u)
    mine, rest, packs, attn_other = lax.optimization_barrier((mine, rest, packs, attn_other))
    half = (mine + core_swap(rest)).astype(BF16)
    others = [core_swap(p) for p in packs]
    half = y_sum(half).astype(BF16)
    *maps, grad = early_pass(me, [pack] + packs, [other] + others, x, u, EARLY)
    half, maps, grad = lax.optimization_barrier((half, maps, grad))
    grad = late_pass(maps, held[1], held[2], grad, EARLY)
    half = z_sum(half, grad)
    fx, mid, out, score, attn = final_pass(me, half, core_swap(half), attn, attn_other)
    return grad.T, fx.T, mid.T, score, attn, out


def solution(mesh):
    fine = Mesh(np.asarray(mesh.devices).reshape(4, 8, 2, 4), PTS + ("head",))
    in_specs = (
        P(PTS, None),
        P(PTS, None),
        P(None, "head"),
        P(None, "head"),
        P("head", None, None),
        P("head"),
        P("head", None, None, None),
        P("head", None),
    )
    out_specs = (
        P(PTS, "head"),
        P(None, "head"),
        P(None, "head"),
        P("head", None, None),
        P("head", None, None, None),
        P("head", None),
    )
    return jax.shard_map(
        per_device, mesh=fine, in_specs=in_specs, out_specs=out_specs, check_vma=False
    )
```
